256 devices in a mesh: gx: 4 (over y), gy: 8 (over z), gz: 8 (over x, core).
Axes of the slice: x: 4, y: 4, z: 8, core: 2. Of those that a mesh axis runs over, the one named last changes fastest.
Arguments:
- adjoint_source: float32 [128, 256, 1024], P('gx', 'gy', 'gz'), may hold values from -6 to 6
- start_guess: float32 [128, 256, 1024], P('gx', 'gy', 'gz'), may hold values from -2 to 2
- phase: float32 [128, 256, 1024], P('gx', 'gy', 'gz'), may hold values from -1.1 to 1.1
- velocity: float32 [128, 256, 1024], P('gx', 'gy', 'gz'), may hold values from -2 to 2
Outputs:
- adjoint: float32 [128, 256, 1024], P('gx', 'gy', 'gz')
- residual: float32 [128, 256, 1024], P('gx', 'gy', 'gz')
The draws below stay inside these ranges and needn't reach their ends.
All inputs are finite; a program needn't handle non-finite values.
Results may differ from the reference program's by a relative error of at most 0.00012.
Values sent between devices are 32-bit elements; how exact they have to be, the bound alone decides.
No kernel may reach another device: no remote copies, remote signals or barrier semaphores. Data moves between devices by JAX's collectives and lax.ppermute only.
A program may use at most 128 MiB of HBM per device.

```python
import jax
import jax.numpy as jnp

ITERS = 3
NX = 128
NY = 256
NZ = 1024


def block_scale(key, shape, shards, low, largest):
    level, own = 1.0, jax.random.fold_in(key, 6)
    for dim, blocks in shards:
        heights = jnp.exp(jax.random.uniform(jax.random.fold_in(own, dim), (blocks,), jnp.float32, low / len(shards), largest / len(shards)))
        level = level * jnp.repeat(heights, shape[dim] // blocks).reshape([-1 if axis == dim else 1 for axis in range(len(shape))])
    return level


def noise(own_key, extent, scale, limit, split=(), kind=jnp.bfloat16):
    values = scale * jax.random.normal(own_key, extent, jnp.float32)
    if split:
        values = values * block_scale(own_key, extent, split, -0.22, 0.18)
    return jnp.clip(values, -limit, limit).astype(kind)


def setup_inputs(seed: int = 0) -> dict:
    key_list = jax.random.split(jax.random.key(seed), 5)
    return {
        "adjoint_source": noise(key_list[0], (NX, NY, NZ), 1.0, 6.0, ((0, 4), (1, 8), (2, 8)), jnp.float32),
        "start_guess": noise(key_list[1], (NX, NY, NZ), 0.3, 2.0, ((0, 4), (1, 8), (2, 8)), jnp.float32),
        "phase": jnp.clip(jax.random.uniform(key_list[2], (NX, NY, NZ), jnp.float32, -1.1, 1.1) * block_scale(key_list[2], (NX, NY, NZ), ((0, 4), (1, 8), (2, 8)), -0.4, 0.0), -1.1, 1.1),
        "velocity": jnp.clip(jax.random.uniform(key_list[3], (NX, NY, NZ), jnp.float32, -2.0, 2.0) * block_scale(key_list[3], (NX, NY, NZ), ((0, 4), (1, 8), (2, 8)), -0.4, 0.0), -2.0, 2.0),
    }


diffuse_coef = 0.05
curv_coef = 0.2
advect_coef = 0.25


def laplace(field):
    padded = jnp.pad(field, ((0, 0), (0, 0), (1, 1)))
    total = padded[:, :, 2:] + padded[:, :, :-2]
    total = total + jnp.roll(field, 1, 0) + jnp.roll(field, -1, 0)
    total = total + jnp.roll(field, 1, 1) + jnp.roll(field, -1, 1)
    return total - 6.0 * field


def operate(field, curvature, velocity):
    lap_one = laplace(field)
    carried = velocity * field
    advect = 0.5 * (jnp.roll(carried, -1, 0) - jnp.roll(carried, 1, 0))
    return field + diffuse_coef * laplace(lap_one) - curv_coef * curvature * lap_one - advect_coef * advect


def reference(adjoint_source, start_guess, phase, velocity):
    curvature = 3.0 * phase * phase - 1.0
    inverse_diag = 1.0 / (1.0 + diffuse_coef * 42.0 + curv_coef * 6.0 * curvature)
    adjoint = start_guess
    residual = adjoint_source - operate(adjoint, curvature, velocity)
    shadow = residual
    search = residual
    shadow_dot = jnp.sum(shadow * residual)
    for step in range(ITERS):
        search_hat = inverse_diag * search
        image = operate(search_hat, curvature, velocity)
        step_len = shadow_dot / jnp.sum(shadow * image)
        middle = residual - step_len * image
        middle_hat = inverse_diag * middle
        second = operate(middle_hat, curvature, velocity)
        stabil = jnp.sum(second * middle) / jnp.sum(second * second)
        adjoint = adjoint + step_len * search_hat + stabil * middle_hat
        residual = middle - stabil * second
        if step + 1 < ITERS:
            new_dot = jnp.sum(shadow * residual)
            blend = (new_dot / shadow_dot) * (step_len / stabil)
            search = residual + blend * (search - stabil * image)
            shadow_dot = new_dot
    return adjoint, residual
```

```python
import jax
import jax.numpy as jnp
from jax import lax
from jax.sharding import PartitionSpec as P

ITERS = 3
STEPS = 2 * ITERS
RESTART = 3
CENTRE = 1.3
RADIUS = 1.3
KAPPA_MAX = 4000.0
AXES = ("gx", "gy", "gz")

diffuse_coef = 0.05
curv_coef = 0.2
advect_coef = 0.25


def extended(value, sides, width):
    for axis, dim in sides:
        peers, length = (lax.axis_size(axis), value.shape[dim])
        up = [(i, (i + 1) % peers) for i in range(peers)]
        down = [(j, i) for i, j in up]
        last = lax.slice_in_dim(value, length - width, length, axis=dim)
        first = lax.slice_in_dim(value, 0, width, axis=dim)
        before = lax.ppermute(last, axis, up)
        after = lax.ppermute(first, axis, down)
        value = jnp.concatenate([before, value, after], axis=dim)
    return value


def wall_mask(width, depth):
    planes = jnp.arange(depth + 2 * width, dtype=jnp.int32)
    global_z = lax.axis_index("gz") * depth + planes - width
    inside = (global_z >= 0) & (global_z < depth * lax.axis_size("gz"))
    return inside.astype(jnp.float32)


def lap_inner(padded):
    total = padded[2:, 1:-1, 1:-1] + padded[:-2, 1:-1, 1:-1]
    total = total + padded[1:-1, 2:, 1:-1] + padded[1:-1, :-2, 1:-1]
    total = total + padded[1:-1, 1:-1, 2:] + padded[1:-1, 1:-1, :-2]
    return total - 6.0 * padded[1:-1, 1:-1, 1:-1]


def operate(field, curvature, vel_rims):
    depth = field.shape[2]
    padded = extended(field, (("gx", 0), ("gy", 1), ("gz", 2)), 2)
    padded = padded * wall_mask(2, depth)
    lap_wide = lap_inner(padded) * wall_mask(1, depth)
    lap_two = lap_inner(lap_wide)
    lap_one = lap_wide[1:-1, 1:-1, 1:-1]
    ahead = padded[3:-1, 2:-2, 2:-2]
    behind = padded[1:-3, 2:-2, 2:-2]
    advect = 0.5 * (vel_rims[2:] * ahead - vel_rims[:-2] * behind)
    return field + diffuse_coef * lap_two - curv_coef * curvature * lap_one - advect_coef * advect


def plain_solve(adjoint_source, start_guess, phase, velocity):
    vel_rims = extended(velocity, (("gx", 0),), 1)
    curvature = 3.0 * phase * phase - 1.0
    inverse_diag = 1.0 / (1.0 + diffuse_coef * 42.0 + curv_coef * 6.0 * curvature)
    adjoint = start_guess
    residual = adjoint_source - operate(adjoint, curvature, vel_rims)
    shadow = residual
    search = residual
    shadow_dot = lax.psum(jnp.sum(shadow * residual), AXES)
    for step in range(ITERS):
        search_hat = inverse_diag * search
        image = operate(search_hat, curvature, vel_rims)
        step_len = shadow_dot / lax.psum(jnp.sum(shadow * image), AXES)
        middle = residual - step_len * image
        middle_hat = inverse_diag * middle
        second = operate(middle_hat, curvature, vel_rims)
        cross, square = lax.psum((jnp.sum(second * middle), jnp.sum(second * second)), AXES)
        stabil = cross / square
        adjoint = adjoint + step_len * search_hat + stabil * middle_hat
        residual = middle - stabil * second
        if step + 1 < ITERS:
            new_dot = lax.psum(jnp.sum(shadow * residual), AXES)
            blend = new_dot / shadow_dot * (step_len / stabil)
            search = residual + blend * (search - stabil * image)
            shadow_dot = new_dot
    return adjoint, residual


def recurrence(k):
    if k % RESTART == 0:
        return 0.0, CENTRE, RADIUS
    return 0.5 * RADIUS, CENTRE, 0.5 * RADIUS


def coefficients(gram):
    def add(*terms):
        total = None
        for factor, value in terms:
            if value is None:
                continue
            piece = value if factor is None else factor * value
            total = piece if total is None else total + piece
        return total

    def apply(vec):
        out = [None] * (STEPS + 1)
        for k in range(STEPS):
            if vec[k] is None:
                continue
            for shift, weight in zip((-1, 0, 1), recurrence(k)):
                if weight:
                    out[k + shift] = add((None, out[k + shift]), (weight, vec[k]))
        return out

    kappa = [jnp.float32(1.0)]

    def dot(a, b):
        total, size = None, None
        for j in range(STEPS + 1):
            if b[j] is None:
                continue
            row, row_size = None, None
            for i in range(STEPS + 1):
                if a[i] is None:
                    continue
                piece = a[i] * gram(min(i, j), max(i, j))
                row = piece if row is None else row + piece
                row_size = jnp.abs(piece) if row_size is None else row_size + jnp.abs(piece)
            total = add((None, total), (b[j], row))
            size = add((None, size), (jnp.abs(b[j]), row_size))
        kappa[0] = jnp.where(size <= KAPPA_MAX * jnp.abs(total), kappa[0], jnp.float32(jnp.inf))
        return total

    def combine(*terms):
        return [add(*((factor, vec[k]) for factor, vec in terms)) for k in range(STEPS + 1)]

    unit = [jnp.float32(1.0)] + [None] * STEPS
    residual, search, shadow = unit, unit, unit
    gain = [None] * (STEPS + 1)
    shadow_dot = dot(shadow, residual)
    for step in range(ITERS):
        image = apply(search)
        step_len = shadow_dot / dot(shadow, image)
        middle = combine((None, residual), (-step_len, image))
        second = apply(middle)
        stabil = dot(second, middle) / dot(second, second)
        gain = combine((None, gain), (step_len, search), (stabil, middle))
        residual = combine((None, middle), (-stabil, second))
        if step + 1 < ITERS:
            new_dot = dot(shadow, residual)
            blend = new_dot / shadow_dot * (step_len / stabil)
            search = combine((None, residual), (blend, search), (-blend * stabil, image))
            shadow_dot = new_dot
    dot(residual, residual)
    zero = jnp.float32(0.0)
    return [zero if g is None else g for g in gain], residual, kappa[0]


def on_device(adjoint_source, start_guess, phase, velocity):
    vel_rims = extended(velocity, (("gx", 0),), 1)
    curvature = 3.0 * phase * phase - 1.0
    inverse_diag = 1.0 / (1.0 + diffuse_coef * 42.0 + curv_coef * 6.0 * curvature)
    basis = [adjoint_source - operate(start_guess, curvature, vel_rims)]
    for k in range(STEPS):
        down, centre, up = recurrence(k)
        image = operate(inverse_diag * basis[k], curvature, vel_rims)
        fresh = (image - centre * basis[k]) * (1.0 / up)
        basis.append(fresh - basis[k - 1] if down else fresh)
    pairs = [(i, j) for i in range(STEPS + 1) for j in range(i, STEPS + 1)]
    sums = jnp.stack([jnp.sum(basis[i] * basis[j]) for i, j in pairs])
    sums = jnp.pad(sums, (0, 128 - len(pairs)))
    parts = lax.all_to_all(jnp.broadcast_to(sums, (lax.axis_size(AXES), 128)), AXES, 0, 0, tiled=True)
    totals = jnp.sum(parts, axis=0)
    gain, tail, kappa = coefficients(lambda i, j: totals[pairs.index((i, j))])

    def combined(_):
        weight = sum(g * q for g, q in zip(gain, basis))
        return start_guess + inverse_diag * weight, sum(t * q for t, q in zip(tail, basis))

    def plain(_):
        return plain_solve(adjoint_source, start_guess, phase, velocity)

    return lax.cond(kappa < jnp.inf, combined, plain, 0)


def solution(mesh):
    placed = P("gx", "gy", "gz")
    return jax.shard_map(on_device, mesh=mesh, in_specs=(placed,) * 4, out_specs=(placed,) * 2, check_vma=False)
```

```python
import functools

import jax
import jax.numpy as jnp
from jax import lax
from jax.experimental import pallas as pl
from jax.experimental.pallas import tpu as pltpu
from jax.sharding import PartitionSpec as P

ITERS = 3
STEPS = 2 * ITERS
RESTART = 3
CENTRE = 1.3
RADIUS = 1.3
KAPPA_MAX = 4000.0
AXES = ("gx", "gy", "gz")
PAIRS = [(i, j) for i in range(STEPS + 1) for j in range(i, STEPS + 1)]
DEEP = 8
COEF = 6
LANES = 128
GROUP = LANES // DEEP

diffuse_coef = 0.05
curv_coef = 0.2
advect_coef = 0.25


def extended(value, sides, width):
    for axis, dim in sides:
        peers, length = (lax.axis_size(axis), value.shape[dim])
        up = [(i, (i + 1) % peers) for i in range(peers)]
        down = [(j, i) for i, j in up]
        last = lax.slice_in_dim(value, length - width, length, axis=dim)
        first = lax.slice_in_dim(value, 0, width, axis=dim)
        before = lax.ppermute(last, axis, up)
        after = lax.ppermute(first, axis, down)
        value = jnp.concatenate([before, value, after], axis=dim)
    return value


def wall_mask(width, depth):
    planes = jnp.arange(depth + 2 * width, dtype=jnp.int32)
    global_z = lax.axis_index("gz") * depth + planes - width
    inside = (global_z >= 0) & (global_z < depth * lax.axis_size("gz"))
    return inside.astype(jnp.float32)


def lap_inner(padded):
    total = padded[2:, 1:-1, 1:-1] + padded[:-2, 1:-1, 1:-1]
    total = total + padded[1:-1, 2:, 1:-1] + padded[1:-1, :-2, 1:-1]
    total = total + padded[1:-1, 1:-1, 2:] + padded[1:-1, 1:-1, :-2]
    return total - 6.0 * padded[1:-1, 1:-1, 1:-1]


def operate(field, curvature, vel_rims):
    depth = field.shape[2]
    padded = extended(field, (("gx", 0), ("gy", 1), ("gz", 2)), 2)
    padded = padded * wall_mask(2, depth)
    lap_wide = lap_inner(padded) * wall_mask(1, depth)
    lap_two = lap_inner(lap_wide)
    lap_one = lap_wide[1:-1, 1:-1, 1:-1]
    ahead = padded[3:-1, 2:-2, 2:-2]
    behind = padded[1:-3, 2:-2, 2:-2]
    advect = 0.5 * (vel_rims[2:] * ahead - vel_rims[:-2] * behind)
    return field + diffuse_coef * lap_two - curv_coef * curvature * lap_one - advect_coef * advect


def plain_solve(adjoint_source, start_guess, phase, velocity):
    vel_rims = extended(velocity, (("gx", 0),), 1)
    curvature = 3.0 * phase * phase - 1.0
    inverse_diag = 1.0 / (1.0 + diffuse_coef * 42.0 + curv_coef * 6.0 * curvature)
    adjoint = start_guess
    residual = adjoint_source - operate(adjoint, curvature, vel_rims)
    shadow = residual
    search = residual
    shadow_dot = lax.psum(jnp.sum(shadow * residual), AXES)
    for step in range(ITERS):
        search_hat = inverse_diag * search
        image = operate(search_hat, curvature, vel_rims)
        step_len = shadow_dot / lax.psum(jnp.sum(shadow * image), AXES)
        middle = residual - step_len * image
        middle_hat = inverse_diag * middle
        second = operate(middle_hat, curvature, vel_rims)
        cross, square = lax.psum((jnp.sum(second * middle), jnp.sum(second * second)), AXES)
        stabil = cross / square
        adjoint = adjoint + step_len * search_hat + stabil * middle_hat
        residual = middle - stabil * second
        if step + 1 < ITERS:
            new_dot = lax.psum(jnp.sum(shadow * residual), AXES)
            blend = new_dot / shadow_dot * (step_len / stabil)
            search = residual + blend * (search - stabil * image)
            shadow_dot = new_dot
    return adjoint, residual


def recurrence(k):
    if k % RESTART == 0:
        return 0.0, CENTRE, RADIUS
    return 0.5 * RADIUS, CENTRE, 0.5 * RADIUS


def coefficients(gram):
    def add(*terms):
        total = None
        for factor, value in terms:
            if value is None:
                continue
            piece = value if factor is None else factor * value
            total = piece if total is None else total + piece
        return total

    def apply(vec):
        out = [None] * (STEPS + 1)
        for k in range(STEPS):
            if vec[k] is None:
                continue
            for shift, weight in zip((-1, 0, 1), recurrence(k)):
                if weight:
                    out[k + shift] = add((None, out[k + shift]), (weight, vec[k]))
        return out

    one = jnp.ones_like(gram(0, 0))
    kappa = [one]

    def dot(a, b):
        total, size = None, None
        for j in range(STEPS + 1):
            if b[j] is None:
                continue
            row, row_size = None, None
            for i in range(STEPS + 1):
                if a[i] is None:
                    continue
                piece = a[i] * gram(min(i, j), max(i, j))
                row = piece if row is None else row + piece
                row_size = jnp.abs(piece) if row_size is None else row_size + jnp.abs(piece)
            total = add((None, total), (b[j], row))
            size = add((None, size), (jnp.abs(b[j]), row_size))
        kappa[0] = jnp.where(size <= KAPPA_MAX * jnp.abs(total), kappa[0], 0.0)
        return total

    def combine(*terms):
        return [add(*((factor, vec[k]) for factor, vec in terms)) for k in range(STEPS + 1)]

    unit = [one] + [None] * STEPS
    residual, search, shadow = unit, unit, unit
    gain = [None] * (STEPS + 1)
    shadow_dot = dot(shadow, residual)
    for step in range(ITERS):
        image = apply(search)
        step_len = shadow_dot / dot(shadow, image)
        middle = combine((None, residual), (-step_len, image))
        second = apply(middle)
        stabil = dot(second, middle) / dot(second, second)
        gain = combine((None, gain), (step_len, search), (stabil, middle))
        residual = combine((None, middle), (-stabil, second))
        if step + 1 < ITERS:
            new_dot = dot(shadow, residual)
            blend = new_dot / shadow_dot * (step_len / stabil)
            search = combine((None, residual), (blend, search), (-blend * stabil, image))
            shadow_dot = new_dot
    dot(residual, residual)
    return gain, residual, kappa[0]


def lanes_of(shape):
    return lax.broadcasted_iota(jnp.int32, shape, len(shape) - 1)


def pack_rows_kernel(parts, own_refs, low_ref, high_ref, to_high_ref, to_low_ref):
    start, at = 0, 0
    for depth, own_ref in zip(parts, own_refs):
        blocks, rows = own_ref.shape[0], own_ref.shape[1]
        for here, ref, size in (
            (start, low_ref, depth),
            (None, own_ref, blocks),
            (start, high_ref, depth),
        ):
            first = 0 if here is None else here
            to_high_ref[at : at + size] = ref[first : first + size, rows - DEEP :, :]
            to_low_ref[at : at + size] = ref[first : first + size, :DEEP, :]
            at += size
        start += depth


def assemble_kernel(parts, own_refs, xlow_ref, xhigh_ref, ylow_ref, yhigh_ref, wide_ref, to_high_ref, to_low_ref):
    start, at = 0, 0
    for a, (depth, own_ref) in enumerate(zip(parts, own_refs)):
        blocks, rows = own_ref.shape[0], own_ref.shape[1]
        wide, tall = blocks + 2 * DEEP, rows + 2 * DEEP
        gap = DEEP - depth
        if gap:
            wide_ref[a, :gap] = jnp.zeros((gap, tall, LANES), jnp.float32)
            wide_ref[a, wide - gap :] = jnp.zeros((gap, tall, LANES), jnp.float32)
        wide_ref[a, gap:DEEP, DEEP : DEEP + rows, :] = xlow_ref[start : start + depth]
        wide_ref[a, DEEP : DEEP + blocks, DEEP : DEEP + rows, :] = own_ref[...]
        wide_ref[a, DEEP + blocks : DEEP + blocks + depth, DEEP : DEEP + rows, :] = xhigh_ref[start : start + depth]
        wide_ref[a, gap : wide - gap, :DEEP, :] = ylow_ref[at : at + wide - 2 * gap]
        wide_ref[a, gap : wide - gap, DEEP + rows :, :] = yhigh_ref[at : at + wide - 2 * gap]
        start += depth
        at += wide - 2 * gap
        lanes = lanes_of((tall, LANES))
        for g in range(wide // GROUP):
            up = jnp.zeros((tall, LANES), jnp.float32)
            down = jnp.zeros((tall, LANES), jnp.float32)
            for i in range(GROUP):
                plane = wide_ref[a, g * GROUP + i]
                chosen = lanes // DEEP == i
                up = jnp.where(chosen, turn(plane, DEEP * (i + 1)), up)
                down = jnp.where(chosen, turn(plane, DEEP * i), down)
            to_high_ref[a, g] = up
            to_low_ref[a, g] = down


def turn(plane, shift, axis=1):
    shift = shift % plane.shape[axis]
    return pltpu.roll(plane, shift, axis) if shift else plane


def unpack(low_ref, high_ref, a, put):
    groups, tall = low_ref.shape[1], low_ref.shape[2]
    lanes = lanes_of((tall, LANES))
    for g in range(groups):
        below, above = low_ref[a, g], high_ref[a, g]
        for i in range(GROUP):
            tile = jnp.where(lanes >= LANES - DEEP, turn(below, -DEEP * (i + 1)), 0.0)
            put(g * GROUP + i, jnp.where(lanes < DEEP, turn(above, -DEEP * i), tile))


def inside_mask(edge_ref, tall):
    lanes = lanes_of((tall, LANES))
    edge = edge_ref[0]
    above = jnp.logical_and(lanes < DEEP, edge != 2)
    below = jnp.logical_and(lanes >= LANES - DEEP, edge != 1)
    return jnp.where(jnp.logical_or(above, below), 1.0, 0.0)


def laplacian(ref, x, lanes):
    mid = [ref[t, x] for t in range(2)]
    ahead = [turn(m, -1) for m in mid]
    behind = [turn(m, 1) for m in mid]
    out = []
    for t in range(2):
        m = mid[t]
        along = jnp.where(lanes == LANES - 1, ahead[1 - t], ahead[t]) + jnp.where(lanes == 0, behind[1 - t], behind[t])
        across = turn(m, 1, 0) + turn(m, -1, 0)
        out.append((ref[t, x - 1] + ref[t, x + 1]) + (across + along) - 6.0 * m)
    return out


def build_coefficients(wide_ref, low_ref, high_ref, mask, at_phase, at_vel, inv_ref, curv_ref, vel_ref):
    wide = wide_ref.shape[1]

    def keep_phase(x, tile):
        curv_ref[1, x] = tile

    def keep_vel(x, tile):
        vel_ref[1, x] = tile

    unpack(low_ref, high_ref, at_phase, keep_phase)
    unpack(low_ref, high_ref, at_vel, keep_vel)

    vel_ref[0] = wide_ref[at_vel]

    @pl.loop(DEEP - COEF, wide - DEEP + COEF)
    def _(x):
        for t in range(2):
            phase = wide_ref[at_phase, x] if t == 0 else curv_ref[1, x]
            curvature = 3.0 * phase * phase - 1.0
            inverse = 1.0 / (1.0 + diffuse_coef * 42.0 + curv_coef * 6.0 * curvature)
            inv_ref[t, x] = inverse if t == 0 else inverse * mask
            curv_ref[t, x] = curv_coef * curvature


def apply_operator(u_ref, lap_ref, curv_ref, vel_ref, mask, first, last, put):
    lanes = lanes_of(mask.shape)

    @pl.loop(first - 1, last + 1)
    def _(x):
        lap = laplacian(u_ref, x, lanes)
        lap_ref[0, x] = lap[0]
        lap_ref[1, x] = lap[1] * mask

    @pl.loop(first, last)
    def _(x):
        twice = laplacian(lap_ref, x, lanes)
        for t in range(2):
            flow = vel_ref[t, x + 1] * u_ref[t, x + 1] - vel_ref[t, x - 1] * u_ref[t, x - 1]
            image = u_ref[t, x] + diffuse_coef * twice[t] - curv_ref[t, x] * lap_ref[t, x] - (0.5 * advect_coef) * flow
            put(t, x, image)


def extend_basis(k, source_ref, older_ref, u_ref, lap_ref, inv_ref, curv_ref, vel_ref, mask, first, last, keep):
    down, centre, up = recurrence(k)

    @pl.loop(first - 2, last + 2)
    def _(x):
        for t in range(2):
            u_ref[t, x] = inv_ref[t, x] * source_ref[t, x]

    def put(t, x, image):
        fresh = (image - centre * source_ref[t, x]) * (1.0 / up)
        if down:
            fresh = fresh - older_ref[t, x]
        older_ref[t, x] = fresh

    apply_operator(u_ref, lap_ref, curv_ref, vel_ref, mask, first, last, put)
    blocks, rows = keep.shape[0], keep.shape[1]
    keep[...] = older_ref[0, DEEP : DEEP + blocks, DEEP : DEEP + rows, :]


def first_half_kernel(edge_ref, wide_ref, low_ref, high_ref, basis_ref, a_ref, b_ref, u_ref, lap_ref, inv_ref, curv_ref, vel_ref):
    wide, tall = wide_ref.shape[1], wide_ref.shape[2]
    blocks, rows = basis_ref.shape[1], basis_ref.shape[2]
    mask = inside_mask(edge_ref, tall)
    build_coefficients(wide_ref, low_ref, high_ref, mask, 2, 3, inv_ref, curv_ref, vel_ref)

    def keep_start(x, tile):
        u_ref[1, x] = tile * mask

    def keep_source(x, tile):
        a_ref[1, x] = tile

    unpack(low_ref, high_ref, 0, keep_start)
    unpack(low_ref, high_ref, 1, keep_source)
    u_ref[0] = wide_ref[0]

    def put(t, x, image):
        a_ref[t, x] = (wide_ref[1, x] if t == 0 else a_ref[1, x]) - image

    apply_operator(u_ref, lap_ref, curv_ref, vel_ref, mask, 2, wide - 2, put)
    basis_ref[0] = a_ref[0, DEEP : DEEP + blocks, DEEP : DEEP + rows, :]
    here, there = a_ref, b_ref
    for k in range(RESTART):
        margin = 2 * (k + 2)
        extend_basis(
            k, here, there, u_ref, lap_ref, inv_ref, curv_ref, vel_ref, mask, margin, wide - margin, basis_ref.at[k + 1]
        )
        here, there = there, here


def second_half_kernel(
    edge_ref, wide_ref, low_ref, high_ref, qwide_ref, qlow_ref, qhigh_ref, older_ref, basis_ref, sums_ref,
    a_ref, b_ref, u_ref, lap_ref, inv_ref, curv_ref, vel_ref,
):
    wide, tall = wide_ref.shape[1], wide_ref.shape[2]
    blocks, rows = older_ref.shape[1], older_ref.shape[2]
    mask = inside_mask(edge_ref, tall)
    build_coefficients(wide_ref, low_ref, high_ref, mask, 2, 3, inv_ref, curv_ref, vel_ref)

    def keep(x, tile):
        a_ref[1, x] = tile

    unpack(qlow_ref, qhigh_ref, 0, keep)
    a_ref[0] = qwide_ref[0]
    here, there = a_ref, b_ref
    for k in range(RESTART, STEPS):
        margin = DEEP - COEF + 2 * (k - RESTART + 1)
        extend_basis(
            k, here, there, u_ref, lap_ref, inv_ref, curv_ref, vel_ref, mask, margin, wide - margin, basis_ref.at[k - RESTART]
        )
        here, there = there, here

    def body(x, sums):
        planes = [older_ref[k, x] for k in range(RESTART + 1)] + [basis_ref[k, x] for k in range(STEPS - RESTART)]
        out = []
        for total, (i, j) in zip(sums, PAIRS):
            out.append(total + jnp.sum((planes[i] * planes[j]).reshape(rows // 8, 8, LANES), axis=0))
        return tuple(out)

    sums = lax.fori_loop(0, blocks, body, tuple(jnp.zeros((8, LANES), jnp.float32) for _ in PAIRS))
    lanes = lanes_of((8, LANES))
    packed = jnp.zeros((8, LANES), jnp.float32)
    for n, total in enumerate(sums):
        packed = jnp.where(lanes == n, jnp.sum(total, axis=1, keepdims=True), packed)
    packed = jnp.sum(packed, axis=0, keepdims=True)
    sums_ref[...] = jnp.broadcast_to(packed, sums_ref.shape)


def combine_kernel(parts_ref, older_ref, newer_ref, start_ref, phase_ref, adjoint_ref, residual_ref, sound_ref):
    blocks, rows = start_ref.shape[0], start_ref.shape[1]
    totals = jnp.sum(parts_ref[...].reshape(-1, 8, LANES), axis=0)
    totals = jnp.broadcast_to(jnp.sum(totals, axis=0, keepdims=True), (8, LANES))
    lanes = lanes_of((8, LANES))
    values = {
        pair: jnp.broadcast_to(jnp.sum(jnp.where(lanes == n, totals, 0.0), axis=1, keepdims=True), (8, LANES))
        for n, pair in enumerate(PAIRS)
    }
    gain, tail, sound = coefficients(lambda i, j: values[i, j])
    sound_ref[...] = sound

    @pl.loop(0, blocks)
    def _(x):
        first, second = None, None
        for k in range(STEPS + 1):
            plane = (older_ref[k, x] if k <= RESTART else newer_ref[k - RESTART - 1, x]).reshape(rows // 8, 8, LANES)
            if gain[k] is not None:
                first = gain[k] * plane if first is None else first + gain[k] * plane
            second = tail[k] * plane if second is None else second + tail[k] * plane
        phase = phase_ref[x]
        curvature = 3.0 * phase * phase - 1.0
        inverse = 1.0 / (1.0 + diffuse_coef * 42.0 + curv_coef * 6.0 * curvature)
        adjoint_ref[x] = start_ref[x] + inverse * first.reshape(rows, LANES)
        residual_ref[x] = second.reshape(rows, LANES)


VMEM = pl.BlockSpec(memory_space=pltpu.VMEM)
SMEM = pl.BlockSpec(memory_space=pltpu.SMEM)


def call(kernel, outs, *args, scratch=(), scalars=0):
    return pl.pallas_call(
        kernel,
        out_shape=[jax.ShapeDtypeStruct(shape, jnp.float32) for shape in outs],
        in_specs=[SMEM] * scalars + [VMEM] * (len(args) - scalars),
        out_specs=[VMEM] * len(outs),
        scratch_shapes=[pltpu.VMEM(shape, jnp.float32) for shape in scratch],
        compiler_params=pltpu.CompilerParams(vmem_limit_bytes=48 * 2**20),
    )(*args)


def swapped(to_high, to_low, axis, wrap):
    peers = lax.axis_size(axis)
    up = [(i, (i + 1) % peers) for i in range(peers if wrap else peers - 1)]
    return lax.ppermute(to_high, axis, up), lax.ppermute(to_low, axis, [(j, i) for i, j in up])


def exchange(owns, parts):
    n = len(parts)
    blocks, rows = owns[0].shape[0], owns[0].shape[1]
    to_high = jnp.concatenate([own[blocks - depth :] for own, depth in zip(owns, parts)])
    to_low = jnp.concatenate([own[:depth] for own, depth in zip(owns, parts)])
    xlow, xhigh = swapped(to_high, to_low, "gx", True)
    lines = (sum(blocks + 2 * depth for depth in parts), DEEP, LANES)

    def pack(*refs):
        pack_rows_kernel(parts, refs[:n], *refs[n:])

    ylow, yhigh = swapped(*call(pack, (lines, lines), *owns, xlow, xhigh), "gy", True)
    wide, tall = blocks + 2 * DEEP, rows + 2 * DEEP

    def assemble(*refs):
        assemble_kernel(parts, refs[:n], *refs[n:])

    ends = (n, wide // GROUP, tall, LANES)
    block, to_high, to_low = call(assemble, ((n, wide, tall, LANES), ends, ends), *owns, xlow, xhigh, ylow, yhigh)
    return (block, *swapped(to_high, to_low, "gz", False))


def on_device(adjoint_source, start_guess, phase, velocity):
    blocks, rows, _ = phase.shape
    place = lax.axis_index("gz")
    edge = jnp.where(place == 0, 1, jnp.where(place == lax.axis_size("gz") - 1, 2, 0)).astype(jnp.int32).reshape(1)
    wide, low, high = exchange([start_guess, adjoint_source, phase, velocity], [DEEP, COEF, COEF, COEF + 1])
    scratch = [(2, blocks + 2 * DEEP, rows + 2 * DEEP, LANES)] * 7
    (older,) = call(
        first_half_kernel, ((RESTART + 1, blocks, rows, LANES),), edge, wide, low, high, scratch=scratch, scalars=1
    )
    qwide, qlow, qhigh = exchange([older[RESTART]], [COEF])
    newer, sums = call(
        second_half_kernel,
        ((STEPS - RESTART, blocks, rows, LANES), (lax.axis_size(AXES), LANES)),
        edge, wide, low, high, qwide, qlow, qhigh, older, scratch=scratch, scalars=1,
    )
    parts = lax.all_to_all(sums, AXES, 0, 0, tiled=True)
    adjoint, residual, sound = call(
        combine_kernel, (phase.shape, phase.shape, (8, LANES)), parts, older, newer, start_guess, phase
    )

    def plain(state):
        return (jnp.float32(1.0), *plain_solve(adjoint_source, start_guess, phase, velocity))

    return lax.while_loop(lambda state: ~(state[0] > 0.5), plain, (sound[0, 0], adjoint, residual))[1:]


def solution(mesh):
    placed = P("gx", "gy", "gz")
    return jax.shard_map(on_device, mesh=mesh, in_specs=(placed,) * 4, out_specs=(placed,) * 2, check_vma=False)
```

```python
import functools

import jax
import jax.numpy as jnp
from jax import lax
from jax.experimental import pallas as pl
from jax.experimental.pallas import tpu as pltpu
from jax.sharding import PartitionSpec as P

ITERS = 3
STEPS = 2 * ITERS
RESTART = 3
CENTRE = 1.3
RADIUS = 1.3
KAPPA_MAX = 4000.0
AXES = ("gx", "gy", "gz")
PAIRS = [(i, j) for i in range(STEPS + 1) for j in range(i, STEPS + 1)]
DEEP = 8
COEF = 6
LANES = 128
PAD = 8
CHUNK = 8
PLANES = 16
GROUP = LANES // DEEP

diffuse_coef = 0.05
curv_coef = 0.2
advect_coef = 0.25


def extended(value, sides, width):
    for axis, dim in sides:
        peers, length = (lax.axis_size(axis), value.shape[dim])
        up = [(i, (i + 1) % peers) for i in range(peers)]
        down = [(j, i) for i, j in up]
        last = lax.slice_in_dim(value, length - width, length, axis=dim)
        first = lax.slice_in_dim(value, 0, width, axis=dim)
        before = lax.ppermute(last, axis, up)
        after = lax.ppermute(first, axis, down)
        value = jnp.concatenate([before, value, after], axis=dim)
    return value


def wall_mask(width, depth):
    planes = jnp.arange(depth + 2 * width, dtype=jnp.int32)
    global_z = lax.axis_index("gz") * depth + planes - width
    inside = (global_z >= 0) & (global_z < depth * lax.axis_size("gz"))
    return inside.astype(jnp.float32)


def lap_inner(padded):
    total = padded[2:, 1:-1, 1:-1] + padded[:-2, 1:-1, 1:-1]
    total = total + padded[1:-1, 2:, 1:-1] + padded[1:-1, :-2, 1:-1]
    total = total + padded[1:-1, 1:-1, 2:] + padded[1:-1, 1:-1, :-2]
    return total - 6.0 * padded[1:-1, 1:-1, 1:-1]


def operate(field, curvature, vel_rims):
    depth = field.shape[2]
    padded = extended(field, (("gx", 0), ("gy", 1), ("gz", 2)), 2)
    padded = padded * wall_mask(2, depth)
    lap_wide = lap_inner(padded) * wall_mask(1, depth)
    lap_two = lap_inner(lap_wide)
    lap_one = lap_wide[1:-1, 1:-1, 1:-1]
    ahead = padded[3:-1, 2:-2, 2:-2]
    behind = padded[1:-3, 2:-2, 2:-2]
    advect = 0.5 * (vel_rims[2:] * ahead - vel_rims[:-2] * behind)
    return field + diffuse_coef * lap_two - curv_coef * curvature * lap_one - advect_coef * advect


def plain_solve(adjoint_source, start_guess, phase, velocity):
    vel_rims = extended(velocity, (("gx", 0),), 1)
    curvature = 3.0 * phase * phase - 1.0
    inverse_diag = 1.0 / (1.0 + diffuse_coef * 42.0 + curv_coef * 6.0 * curvature)
    adjoint = start_guess
    residual = adjoint_source - operate(adjoint, curvature, vel_rims)
    shadow = residual
    search = residual
    shadow_dot = lax.psum(jnp.sum(shadow * residual), AXES)
    for step in range(ITERS):
        search_hat = inverse_diag * search
        image = operate(search_hat, curvature, vel_rims)
        step_len = shadow_dot / lax.psum(jnp.sum(shadow * image), AXES)
        middle = residual - step_len * image
        middle_hat = inverse_diag * middle
        second = operate(middle_hat, curvature, vel_rims)
        cross, square = lax.psum((jnp.sum(second * middle), jnp.sum(second * second)), AXES)
        stabil = cross / square
        adjoint = adjoint + step_len * search_hat + stabil * middle_hat
        residual = middle - stabil * second
        if step + 1 < ITERS:
            new_dot = lax.psum(jnp.sum(shadow * residual), AXES)
            blend = new_dot / shadow_dot * (step_len / stabil)
            search = residual + blend * (search - stabil * image)
            shadow_dot = new_dot
    return adjoint, residual


def recurrence(k):
    if k % RESTART == 0:
        return 0.0, CENTRE, RADIUS
    return 0.5 * RADIUS, CENTRE, 0.5 * RADIUS


def coefficients(gram):
    def add(*terms):
        total = None
        for factor, value in terms:
            if value is None:
                continue
            piece = value if factor is None else factor * value
            total = piece if total is None else total + piece
        return total

    def apply(vec):
        out = [None] * (STEPS + 1)
        for k in range(STEPS):
            if vec[k] is None:
                continue
            for shift, weight in zip((-1, 0, 1), recurrence(k)):
                if weight:
                    out[k + shift] = add((None, out[k + shift]), (weight, vec[k]))
        return out

    one = jnp.ones_like(gram(0, 0))
    kappa = [one]

    def dot(a, b):
        total, size = None, None
        for j in range(STEPS + 1):
            if b[j] is None:
                continue
            row, row_size = None, None
            for i in range(STEPS + 1):
                if a[i] is None:
                    continue
                piece = a[i] * gram(min(i, j), max(i, j))
                row = piece if row is None else row + piece
                row_size = jnp.abs(piece) if row_size is None else row_size + jnp.abs(piece)
            total = add((None, total), (b[j], row))
            size = add((None, size), (jnp.abs(b[j]), row_size))
        kappa[0] = jnp.where(size <= KAPPA_MAX * jnp.abs(total), kappa[0], 0.0)
        return total

    def combine(*terms):
        return [add(*((factor, vec[k]) for factor, vec in terms)) for k in range(STEPS + 1)]

    unit = [one] + [None] * STEPS
    residual, search, shadow = unit, unit, unit
    gain = [None] * (STEPS + 1)
    shadow_dot = dot(shadow, residual)
    for step in range(ITERS):
        image = apply(search)
        step_len = shadow_dot / dot(shadow, image)
        middle = combine((None, residual), (-step_len, image))
        second = apply(middle)
        stabil = dot(second, middle) / dot(second, second)
        gain = combine((None, gain), (step_len, search), (stabil, middle))
        residual = combine((None, middle), (-stabil, second))
        if step + 1 < ITERS:
            new_dot = dot(shadow, residual)
            blend = new_dot / shadow_dot * (step_len / stabil)
            search = combine((None, residual), (blend, search), (-blend * stabil, image))
            shadow_dot = new_dot
    dot(residual, residual)
    return gain, residual, kappa[0]


def lanes_of(shape):
    return lax.broadcasted_iota(jnp.int32, shape, len(shape) - 1)


def pack_rows_kernel(parts, own_refs, low_ref, high_ref, to_high_ref, to_low_ref):
    start, at = 0, 0
    for depth, own_ref in zip(parts, own_refs):
        blocks, rows = own_ref.shape[0], own_ref.shape[1]
        for here, ref, size in (
            (start, low_ref, depth),
            (None, own_ref, blocks),
            (start, high_ref, depth),
        ):
            first = 0 if here is None else here
            to_high_ref[at : at + size] = ref[first : first + size, rows - DEEP :, :]
            to_low_ref[at : at + size] = ref[first : first + size, :DEEP, :]
            at += size
        start += depth


def assemble_kernel(parts, own_refs, xlow_ref, xhigh_ref, ylow_ref, yhigh_ref, wide_ref, to_high_ref, to_low_ref):
    start, at = 0, 0
    for a, (depth, own_ref) in enumerate(zip(parts, own_refs)):
        blocks, rows = own_ref.shape[0], own_ref.shape[1]
        wide, tall = blocks + 2 * DEEP, rows + 2 * DEEP
        gap = DEEP - depth
        if gap:
            wide_ref[a, :gap] = jnp.zeros((gap, tall, LANES), jnp.float32)
            wide_ref[a, wide - gap :] = jnp.zeros((gap, tall, LANES), jnp.float32)
        wide_ref[a, gap:DEEP, DEEP : DEEP + rows, :] = xlow_ref[start : start + depth]
        wide_ref[a, DEEP : DEEP + blocks, DEEP : DEEP + rows, :] = own_ref[...]
        wide_ref[a, DEEP + blocks : DEEP + blocks + depth, DEEP : DEEP + rows, :] = xhigh_ref[start : start + depth]
        wide_ref[a, gap : wide - gap, :DEEP, :] = ylow_ref[at : at + wide - 2 * gap]
        wide_ref[a, gap : wide - gap, DEEP + rows :, :] = yhigh_ref[at : at + wide - 2 * gap]
        start += depth
        at += wide - 2 * gap
        lanes = lanes_of((tall, LANES))
        for g in range(wide // GROUP):
            up = jnp.zeros((tall, LANES), jnp.float32)
            down = jnp.zeros((tall, LANES), jnp.float32)
            for i in range(GROUP):
                plane = wide_ref[a, g * GROUP + i]
                chosen = lanes // DEEP == i
                up = jnp.where(chosen, turn(plane, DEEP * (i + 1)), up)
                down = jnp.where(chosen, turn(plane, DEEP * i), down)
            to_high_ref[a, g] = up
            to_low_ref[a, g] = down


def turn(plane, shift, axis=1):
    shift = shift % plane.shape[axis]
    return pltpu.roll(plane, shift, axis) if shift else plane


def unpack(low_ref, high_ref, a, put):
    groups, tall = low_ref.shape[1], low_ref.shape[2]
    lanes = lanes_of((tall, LANES))
    for g in range(groups):
        below, above = low_ref[a, g], high_ref[a, g]
        for i in range(GROUP):
            tile = jnp.where(lanes >= LANES - DEEP, turn(below, -DEEP * (i + 1)), 0.0)
            put(g * GROUP + i, jnp.where(lanes < DEEP, turn(above, -DEEP * i), tile))


def inside_mask(edge_ref, tall):
    lanes = lanes_of((tall, LANES))
    edge = edge_ref[0]
    above = jnp.logical_and(lanes < DEEP, edge != 2)
    below = jnp.logical_and(lanes >= LANES - DEEP, edge != 1)
    return jnp.where(jnp.logical_or(above, below), 1.0, 0.0)


def laplacian(ref, x, y, size, lanes):
    here = pl.ds(PAD + y, size)
    mid = [ref[t, x, here, :] for t in range(2)]
    ahead = [turn(m, -1) for m in mid]
    behind = [turn(m, 1) for m in mid]
    out = []
    for t in range(2):
        along = jnp.where(lanes == LANES - 1, ahead[1 - t], ahead[t]) + jnp.where(lanes == 0, behind[1 - t], behind[t])
        across = ref[t, x, pl.ds(PAD + y - 1, size), :] + ref[t, x, pl.ds(PAD + y + 1, size), :]
        out.append((ref[t, x - 1, here, :] + ref[t, x + 1, here, :]) + (across + along) - 6.0 * mid[t])
    return out


def build_coefficients(wide_ref, low_ref, high_ref, mask, at_phase, at_vel, inv_ref, curv_ref, vel_ref):
    wide = wide_ref.shape[1]

    def keep_phase(x, tile):
        curv_ref[1, x] = tile

    def keep_vel(x, tile):
        vel_ref[1, x] = tile

    unpack(low_ref, high_ref, at_phase, keep_phase)
    unpack(low_ref, high_ref, at_vel, keep_vel)

    vel_ref[0] = wide_ref[at_vel]

    @pl.loop(DEEP - COEF, wide - DEEP + COEF, unroll=4)
    def _(x):
        for t in range(2):
            phase = wide_ref[at_phase, x] if t == 0 else curv_ref[1, x]
            curvature = 3.0 * phase * phase - 1.0
            inverse = 1.0 / (1.0 + diffuse_coef * 42.0 + curv_coef * 6.0 * curvature)
            inv_ref[t, x] = inverse if t == 0 else inverse * mask
            curv_ref[t, x] = curv_coef * curvature


def steps(first, last, planes, rows, size, body):
    count = (last - first) // planes

    def chunk(start, n):
        for y in range(*rows, size):
            stores = []
            for j in range(n):
                stores += body(start + j, y)
            for store in stores:
                store()

    @pl.loop(0, count)
    def _(i):
        chunk(first + i * planes, planes)

    if first + count * planes < last:
        chunk(first + count * planes, last - first - count * planes)


def writer(ref, index, value):
    def store():
        ref[index] = value

    return store


def apply_operator(u_ref, lap_ref, curv_ref, vel_ref, mask, first, last, put):
    tall = curv_ref.shape[2]
    lanes = lanes_of((CHUNK, LANES))
    mask = mask[:CHUNK]

    def lap_part(x, y):
        lap = laplacian(u_ref, x, y, CHUNK, lanes)
        lap[1] = lap[1] * mask
        return [writer(lap_ref, (t, x, pl.ds(PAD + y, CHUNK)), lap[t]) for t in range(2)]

    steps(first - 1, last + 1, PLANES, (0, tall), CHUNK, lap_part)

    def image_part(x, y):
        twice = laplacian(lap_ref, x, y, CHUNK, lanes)
        out = []
        mine, wide = pl.ds(y, CHUNK), pl.ds(PAD + y, CHUNK)
        for t in range(2):
            flow = vel_ref[t, x + 1, mine] * u_ref[t, x + 1, wide] - vel_ref[t, x - 1, mine] * u_ref[t, x - 1, wide]
            image = (u_ref[t, x, wide] + diffuse_coef * twice[t]) - (
                curv_ref[t, x, mine] * lap_ref[t, x, wide] + (0.5 * advect_coef) * flow
            )
            out.append(put(t, x, mine, image))
        return out

    low = first // 8 * 8
    steps(first, last, PLANES, (low, tall - low), CHUNK, image_part)


def extend_basis(k, source_ref, older_ref, u_ref, lap_ref, inv_ref, curv_ref, vel_ref, mask, first, last, keep):
    down, centre, up = recurrence(k)
    tall = curv_ref.shape[2]

    def scale(x, y):
        mine = pl.ds(y, CHUNK)
        return [
            writer(u_ref, (t, x, pl.ds(PAD + y, CHUNK)), inv_ref[t, x, mine] * source_ref[t, x, mine]) for t in range(2)
        ]

    steps(first - 2, last + 2, PLANES, (0, tall), CHUNK, scale)

    def put(t, x, mine, image):
        fresh = (image - centre * source_ref[t, x, mine]) * (1.0 / up)
        if down:
            fresh = fresh - older_ref[t, x, mine]
        return writer(older_ref, (t, x, mine), fresh)

    apply_operator(u_ref, lap_ref, curv_ref, vel_ref, mask, first, last, put)
    blocks, rows = keep.shape[0], keep.shape[1]
    keep[...] = older_ref[0, DEEP : DEEP + blocks, DEEP : DEEP + rows, :]


def first_half_kernel(edge_ref, wide_ref, low_ref, high_ref, basis_ref, a_ref, b_ref, u_ref, lap_ref, inv_ref, curv_ref, vel_ref):
    wide, tall = wide_ref.shape[1], wide_ref.shape[2]
    blocks, rows = basis_ref.shape[1], basis_ref.shape[2]
    mask = inside_mask(edge_ref, tall)
    build_coefficients(wide_ref, low_ref, high_ref, mask, 2, 3, inv_ref, curv_ref, vel_ref)

    def keep_start(x, tile):
        u_ref[1, x, PAD : PAD + tall] = tile * mask

    def keep_source(x, tile):
        a_ref[1, x] = tile

    unpack(low_ref, high_ref, 0, keep_start)
    unpack(low_ref, high_ref, 1, keep_source)
    u_ref[0, :, PAD : PAD + tall, :] = wide_ref[0]

    def put(t, x, mine, image):
        return writer(a_ref, (t, x, mine), (wide_ref[1, x, mine] if t == 0 else a_ref[1, x, mine]) - image)

    apply_operator(u_ref, lap_ref, curv_ref, vel_ref, mask, 2, wide - 2, put)
    basis_ref[0] = a_ref[0, DEEP : DEEP + blocks, DEEP : DEEP + rows, :]
    here, there = a_ref, b_ref
    for k in range(RESTART):
        margin = 2 * (k + 2)
        extend_basis(
            k, here, there, u_ref, lap_ref, inv_ref, curv_ref, vel_ref, mask, margin, wide - margin, basis_ref.at[k + 1]
        )
        here, there = there, here


def second_half_kernel(
    edge_ref, wide_ref, low_ref, high_ref, qwide_ref, qlow_ref, qhigh_ref, older_ref, basis_ref, sums_ref,
    a_ref, b_ref, u_ref, lap_ref, inv_ref, curv_ref, vel_ref,
):
    wide, tall = wide_ref.shape[1], wide_ref.shape[2]
    blocks, rows = older_ref.shape[1], older_ref.shape[2]
    mask = inside_mask(edge_ref, tall)
    build_coefficients(wide_ref, low_ref, high_ref, mask, 2, 3, inv_ref, curv_ref, vel_ref)

    def keep(x, tile):
        a_ref[1, x] = tile

    unpack(qlow_ref, qhigh_ref, 0, keep)
    a_ref[0] = qwide_ref[0]
    here, there = a_ref, b_ref
    for k in range(RESTART, STEPS):
        margin = DEEP - COEF + 2 * (k - RESTART + 1)
        extend_basis(
            k, here, there, u_ref, lap_ref, inv_ref, curv_ref, vel_ref, mask, margin, wide - margin, basis_ref.at[k - RESTART]
        )
        here, there = there, here

    def body(x, sums):
        planes = [older_ref[k, x] for k in range(RESTART + 1)] + [basis_ref[k, x] for k in range(STEPS - RESTART)]
        out = []
        for total, (i, j) in zip(sums, PAIRS):
            out.append(total + jnp.sum((planes[i] * planes[j]).reshape(rows // 8, 8, LANES), axis=0))
        return tuple(out)

    sums = lax.fori_loop(0, blocks, body, tuple(jnp.zeros((8, LANES), jnp.float32) for _ in PAIRS))
    lanes = lanes_of((8, LANES))
    packed = jnp.zeros((8, LANES), jnp.float32)
    for n, total in enumerate(sums):
        packed = jnp.where(lanes == n, jnp.sum(total, axis=1, keepdims=True), packed)
    packed = jnp.sum(packed, axis=0, keepdims=True)
    sums_ref[...] = jnp.broadcast_to(packed, sums_ref.shape)


def combine_kernel(parts_ref, older_ref, newer_ref, start_ref, phase_ref, adjoint_ref, residual_ref, sound_ref):
    blocks, rows = start_ref.shape[0], start_ref.shape[1]
    totals = jnp.sum(parts_ref[...].reshape(-1, 8, LANES), axis=0)
    totals = jnp.broadcast_to(jnp.sum(totals, axis=0, keepdims=True), (8, LANES))
    lanes = lanes_of((8, LANES))
    values = {
        pair: jnp.broadcast_to(jnp.sum(jnp.where(lanes == n, totals, 0.0), axis=1, keepdims=True), (8, LANES))
        for n, pair in enumerate(PAIRS)
    }
    gain, tail, sound = coefficients(lambda i, j: values[i, j])
    sound_ref[...] = sound

    @pl.loop(0, blocks)
    def _(x):
        first, second = None, None
        for k in range(STEPS + 1):
            plane = (older_ref[k, x] if k <= RESTART else newer_ref[k - RESTART - 1, x]).reshape(rows // 8, 8, LANES)
            if gain[k] is not None:
                first = gain[k] * plane if first is None else first + gain[k] * plane
            second = tail[k] * plane if second is None else second + tail[k] * plane
        phase = phase_ref[x]
        curvature = 3.0 * phase * phase - 1.0
        inverse = 1.0 / (1.0 + diffuse_coef * 42.0 + curv_coef * 6.0 * curvature)
        adjoint_ref[x] = start_ref[x] + inverse * first.reshape(rows, LANES)
        residual_ref[x] = second.reshape(rows, LANES)


VMEM = pl.BlockSpec(memory_space=pltpu.VMEM)
SMEM = pl.BlockSpec(memory_space=pltpu.SMEM)


def call(kernel, outs, *args, scratch=(), scalars=0):
    return pl.pallas_call(
        kernel,
        out_shape=[jax.ShapeDtypeStruct(shape, jnp.float32) for shape in outs],
        in_specs=[SMEM] * scalars + [VMEM] * (len(args) - scalars),
        out_specs=[VMEM] * len(outs),
        scratch_shapes=[pltpu.VMEM(shape, jnp.float32) for shape in scratch],
        compiler_params=pltpu.CompilerParams(vmem_limit_bytes=48 * 2**20),
    )(*args)


def swapped(to_high, to_low, axis, wrap):
    peers = lax.axis_size(axis)
    up = [(i, (i + 1) % peers) for i in range(peers if wrap else peers - 1)]
    return lax.ppermute(to_high, axis, up), lax.ppermute(to_low, axis, [(j, i) for i, j in up])


def exchange(owns, parts):
    n = len(parts)
    blocks, rows = owns[0].shape[0], owns[0].shape[1]
    to_high = jnp.concatenate([own[blocks - depth :] for own, depth in zip(owns, parts)])
    to_low = jnp.concatenate([own[:depth] for own, depth in zip(owns, parts)])
    xlow, xhigh = swapped(to_high, to_low, "gx", True)
    lines = (sum(blocks + 2 * depth for depth in parts), DEEP, LANES)

    def pack(*refs):
        pack_rows_kernel(parts, refs[:n], *refs[n:])

    ylow, yhigh = swapped(*call(pack, (lines, lines), *owns, xlow, xhigh), "gy", True)
    wide, tall = blocks + 2 * DEEP, rows + 2 * DEEP

    def assemble(*refs):
        assemble_kernel(parts, refs[:n], *refs[n:])

    ends = (n, wide // GROUP, tall, LANES)
    block, to_high, to_low = call(assemble, ((n, wide, tall, LANES), ends, ends), *owns, xlow, xhigh, ylow, yhigh)
    return (block, *swapped(to_high, to_low, "gz", False))


def on_device(adjoint_source, start_guess, phase, velocity):
    blocks, rows, _ = phase.shape
    place = lax.axis_index("gz")
    edge = jnp.where(place == 0, 1, jnp.where(place == lax.axis_size("gz") - 1, 2, 0)).astype(jnp.int32).reshape(1)
    wide, low, high = exchange([start_guess, adjoint_source, phase, velocity], [DEEP, COEF, COEF, COEF + 1])
    scratch = [(2, blocks + 2 * DEEP, rows + 2 * DEEP + 2 * PAD * (2 <= n < 4), LANES) for n in range(7)]

    (older,) = call(
        first_half_kernel, ((RESTART + 1, blocks, rows, LANES),), edge, wide, low, high, scratch=scratch, scalars=1
    )
    qwide, qlow, qhigh = exchange([older[RESTART]], [COEF])
    newer, sums = call(
        second_half_kernel,
        ((STEPS - RESTART, blocks, rows, LANES), (lax.axis_size(AXES), LANES)),
        edge, wide, low, high, qwide, qlow, qhigh, older, scratch=scratch, scalars=1,
    )
    parts = lax.all_to_all(sums, AXES, 0, 0, tiled=True)
    adjoint, residual, sound = call(
        combine_kernel, (phase.shape, phase.shape, (8, LANES)), parts, older, newer, start_guess, phase
    )

    def plain(state):
        return (jnp.float32(1.0), *plain_solve(adjoint_source, start_guess, phase, velocity))

    return lax.while_loop(lambda state: ~(state[0] > 0.5), plain, (sound[0, 0], adjoint, residual))[1:]


def solution(mesh):
    placed = P("gx", "gy", "gz")
    return jax.shard_map(on_device, mesh=mesh, in_specs=(placed,) * 4, out_specs=(placed,) * 2, check_vma=False)
```

```python
import functools

import jax
import jax.numpy as jnp
from jax import lax
from jax.experimental import pallas as pl
from jax.experimental.pallas import tpu as pltpu
from jax.sharding import PartitionSpec as P

ITERS = 3
STEPS = 2 * ITERS
RESTART = 3
CENTRE = 1.3
RADIUS = 1.3
KAPPA_MAX = 4000.0
AXES = ("gx", "gy", "gz")
PAIRS = [(i, j) for i in range(STEPS + 1) for j in range(i, STEPS + 1)]
DEEP = 8
COEF = 6
LANES = 128
PAD = 8
CHUNK = 8
PLANES = 16
PARTS = (DEEP, COEF, COEF, COEF + 1)
GROUP = LANES // DEEP

diffuse_coef = 0.05
curv_coef = 0.2
advect_coef = 0.25


def extended(value, sides, width):
    for axis, dim in sides:
        peers, length = (lax.axis_size(axis), value.shape[dim])
        up = [(i, (i + 1) % peers) for i in range(peers)]
        down = [(j, i) for i, j in up]
        last = lax.slice_in_dim(value, length - width, length, axis=dim)
        first = lax.slice_in_dim(value, 0, width, axis=dim)
        before = lax.ppermute(last, axis, up)
        after = lax.ppermute(first, axis, down)
        value = jnp.concatenate([before, value, after], axis=dim)
    return value


def wall_mask(width, depth):
    planes = jnp.arange(depth + 2 * width, dtype=jnp.int32)
    global_z = lax.axis_index("gz") * depth + planes - width
    inside = (global_z >= 0) & (global_z < depth * lax.axis_size("gz"))
    return inside.astype(jnp.float32)


def lap_inner(padded):
    total = padded[2:, 1:-1, 1:-1] + padded[:-2, 1:-1, 1:-1]
    total = total + padded[1:-1, 2:, 1:-1] + padded[1:-1, :-2, 1:-1]
    total = total + padded[1:-1, 1:-1, 2:] + padded[1:-1, 1:-1, :-2]
    return total - 6.0 * padded[1:-1, 1:-1, 1:-1]


def operate(field, curvature, vel_rims):
    depth = field.shape[2]
    padded = extended(field, (("gx", 0), ("gy", 1), ("gz", 2)), 2)
    padded = padded * wall_mask(2, depth)
    lap_wide = lap_inner(padded) * wall_mask(1, depth)
    lap_two = lap_inner(lap_wide)
    lap_one = lap_wide[1:-1, 1:-1, 1:-1]
    ahead = padded[3:-1, 2:-2, 2:-2]
    behind = padded[1:-3, 2:-2, 2:-2]
    advect = 0.5 * (vel_rims[2:] * ahead - vel_rims[:-2] * behind)
    return field + diffuse_coef * lap_two - curv_coef * curvature * lap_one - advect_coef * advect


def plain_solve(adjoint_source, start_guess, phase, velocity):
    vel_rims = extended(velocity, (("gx", 0),), 1)
    curvature = 3.0 * phase * phase - 1.0
    inverse_diag = 1.0 / (1.0 + diffuse_coef * 42.0 + curv_coef * 6.0 * curvature)
    adjoint = start_guess
    residual = adjoint_source - operate(adjoint, curvature, vel_rims)
    shadow = residual
    search = residual
    shadow_dot = lax.psum(jnp.sum(shadow * residual), AXES)
    for step in range(ITERS):
        search_hat = inverse_diag * search
        image = operate(search_hat, curvature, vel_rims)
        step_len = shadow_dot / lax.psum(jnp.sum(shadow * image), AXES)
        middle = residual - step_len * image
        middle_hat = inverse_diag * middle
        second = operate(middle_hat, curvature, vel_rims)
        cross, square = lax.psum((jnp.sum(second * middle), jnp.sum(second * second)), AXES)
        stabil = cross / square
        adjoint = adjoint + step_len * search_hat + stabil * middle_hat
        residual = middle - stabil * second
        if step + 1 < ITERS:
            new_dot = lax.psum(jnp.sum(shadow * residual), AXES)
            blend = new_dot / shadow_dot * (step_len / stabil)
            search = residual + blend * (search - stabil * image)
            shadow_dot = new_dot
    return adjoint, residual


def recurrence(k):
    if k % RESTART == 0:
        return 0.0, CENTRE, RADIUS
    return 0.5 * RADIUS, CENTRE, 0.5 * RADIUS


def coefficients(gram):
    def add(*terms):
        total = None
        for factor, value in terms:
            if value is None:
                continue
            piece = value if factor is None else factor * value
            total = piece if total is None else total + piece
        return total

    def apply(vec):
        out = [None] * (STEPS + 1)
        for k in range(STEPS):
            if vec[k] is None:
                continue
            for shift, weight in zip((-1, 0, 1), recurrence(k)):
                if weight:
                    out[k + shift] = add((None, out[k + shift]), (weight, vec[k]))
        return out

    one = jnp.ones_like(gram(0, 0))
    kappa = [one]

    def dot(a, b):
        total, size = None, None
        for j in range(STEPS + 1):
            if b[j] is None:
                continue
            row, row_size = None, None
            for i in range(STEPS + 1):
                if a[i] is None:
                    continue
                piece = a[i] * gram(min(i, j), max(i, j))
                row = piece if row is None else row + piece
                row_size = jnp.abs(piece) if row_size is None else row_size + jnp.abs(piece)
            total = add((None, total), (b[j], row))
            size = add((None, size), (jnp.abs(b[j]), row_size))
        kappa[0] = jnp.where(size <= KAPPA_MAX * jnp.abs(total), kappa[0], 0.0)
        return total

    def combine(*terms):
        return [add(*((factor, vec[k]) for factor, vec in terms)) for k in range(STEPS + 1)]

    unit = [one] + [None] * STEPS
    residual, search, shadow = unit, unit, unit
    gain = [None] * (STEPS + 1)
    shadow_dot = dot(shadow, residual)
    for step in range(ITERS):
        image = apply(search)
        step_len = shadow_dot / dot(shadow, image)
        middle = combine((None, residual), (-step_len, image))
        second = apply(middle)
        stabil = dot(second, middle) / dot(second, second)
        gain = combine((None, gain), (step_len, search), (stabil, middle))
        residual = combine((None, middle), (-stabil, second))
        if step + 1 < ITERS:
            new_dot = dot(shadow, residual)
            blend = new_dot / shadow_dot * (step_len / stabil)
            search = combine((None, residual), (blend, search), (-blend * stabil, image))
            shadow_dot = new_dot
    dot(residual, residual)
    return gain, residual, kappa[0]


def lanes_of(shape):
    return lax.broadcasted_iota(jnp.int32, shape, len(shape) - 1)


def x_first(depth, start, at, own, xlow, xhigh, ylow, yhigh):
    blocks, gap = own.shape[0], DEEP - depth

    def plane(x):
        n = x - gap
        if not 0 <= n < blocks + 2 * depth:
            return None
        if n < depth:
            middle = xlow[start + n]
        elif n < depth + blocks:
            middle = own[n - depth]
        else:
            middle = xhigh[start + n - depth - blocks]
        return jnp.concatenate([ylow[at + n], middle, yhigh[at + n]], axis=0)

    return plane


def y_first(depth, start, at, own, xlow, xhigh, ylow, yhigh):
    blocks, gap = own.shape[0], DEEP - depth

    def plane(x):
        n = x - gap
        if not 0 <= n < blocks + 2 * depth:
            return None
        if n < depth:
            return xlow[start + n]
        if n >= depth + blocks:
            return xhigh[start + n - depth - blocks]
        m = n - depth
        return jnp.concatenate([ylow[at + m], own[m], yhigh[at + m]], axis=0)

    return plane


def pack_rows(parts, owns, low, high, to_high, to_low):
    start, at = 0, 0
    for depth, own in zip(parts, owns):
        blocks, rows = own.shape[0], own.shape[1]
        for first, ref, size in ((start, low, depth), (0, own, blocks), (start, high, depth)):
            to_high[at : at + size] = ref[first : first + size, rows - DEEP :, :]
            to_low[at : at + size] = ref[first : first + size, :DEEP, :]
            at += size
        start += depth


def pack_planes(parts, owns, low, high, to_high, to_low):
    start, at = 0, 0
    for depth, own in zip(parts, owns):
        blocks = own.shape[0]
        for n in range(depth):
            for first, ref in ((0, to_low), (blocks - depth, to_high)):
                m = first + n
                ref[start + n] = jnp.concatenate([low[at + m], own[m], high[at + m]], axis=0)
        start += depth
        at += blocks


def pack_ends(planes, to_high, to_low):
    groups, tall = to_high.shape[1], to_high.shape[2]
    lanes = lanes_of((tall, LANES))
    for a, plane in enumerate(planes):
        for g in range(groups):
            up = jnp.zeros((tall, LANES), jnp.float32)
            down = jnp.zeros((tall, LANES), jnp.float32)
            for i in range(GROUP):
                value = plane(g * GROUP + i)
                if value is None:
                    continue
                chosen = lanes // DEEP == i
                up = jnp.where(chosen, turn(value, DEEP * (i + 1)), up)
                down = jnp.where(chosen, turn(value, DEEP * i), down)
            to_high[a, g] = up
            to_low[a, g] = down


def start_kernel(one, two, three, four, xa_high, xa_low, yb_high, yb_low):
    blocks, rows = one.shape[0], one.shape[1]
    at = 0
    for depth, own in zip(PARTS[:2], (one, two)):
        xa_high[at : at + depth] = own[blocks - depth :]
        xa_low[at : at + depth] = own[:depth]
        at += depth
    for n, own in enumerate((three, four)):
        yb_high[n * blocks : (n + 1) * blocks] = own[:, rows - DEEP :, :]
        yb_low[n * blocks : (n + 1) * blocks] = own[:, :DEEP, :]


def turn_kernel(one, two, three, four, xalow, xahigh, yblow, ybhigh, ya_high, ya_low, xb_high, xb_low):
    pack_rows(PARTS[:2], (one, two), xalow, xahigh, ya_high, ya_low)
    pack_planes(PARTS[2:], (three, four), yblow, ybhigh, xb_high, xb_low)


def planes_of(owns, halos):
    xalow, xahigh, yblow, ybhigh, yalow, yahigh, xblow, xbhigh = halos
    blocks = owns[0].shape[0]
    first = [
        x_first(PARTS[0], 0, 0, owns[0], xalow, xahigh, yalow, yahigh),
        x_first(PARTS[1], PARTS[0], blocks + 2 * PARTS[0], owns[1], xalow, xahigh, yalow, yahigh),
    ]
    return first + [
        y_first(PARTS[2], 0, 0, owns[2], xblow, xbhigh, yblow, ybhigh),
        y_first(PARTS[3], PARTS[2], blocks, owns[3], xblow, xbhigh, yblow, ybhigh),
    ]


def fill(plane, count, put):
    for x in range(count):
        value = plane(x)
        if value is not None:
            put(x, value)


def turn(plane, shift, axis=1):
    shift = shift % plane.shape[axis]
    return pltpu.roll(plane, shift, axis) if shift else plane


def unpack(low_ref, high_ref, a, put):
    groups, tall = low_ref.shape[1], low_ref.shape[2]
    lanes = lanes_of((tall, LANES))
    for g in range(groups):
        below, above = low_ref[a, g], high_ref[a, g]
        for i in range(GROUP):
            tile = jnp.where(lanes >= LANES - DEEP, turn(below, -DEEP * (i + 1)), 0.0)
            put(g * GROUP + i, jnp.where(lanes < DEEP, turn(above, -DEEP * i), tile))


def inside_mask(edge_ref, tall):
    lanes = lanes_of((tall, LANES))
    edge = edge_ref[0]
    above = jnp.logical_and(lanes < DEEP, edge != 2)
    below = jnp.logical_and(lanes >= LANES - DEEP, edge != 1)
    return jnp.where(jnp.logical_or(above, below), 1.0, 0.0)


def laplacian(ref, x, y, size, lanes):
    here = pl.ds(PAD + y, size)
    mid = [ref[t, x, here, :] for t in range(2)]
    ahead = [turn(m, -1) for m in mid]
    behind = [turn(m, 1) for m in mid]
    out = []
    for t in range(2):
        along = jnp.where(lanes == LANES - 1, ahead[1 - t], ahead[t]) + jnp.where(lanes == 0, behind[1 - t], behind[t])
        across = ref[t, x, pl.ds(PAD + y - 1, size), :] + ref[t, x, pl.ds(PAD + y + 1, size), :]
        out.append((ref[t, x - 1, here, :] + ref[t, x + 1, here, :]) + (across + along) - 6.0 * mid[t])
    return out


def build_coefficients(planes, low_ref, high_ref, mask, inv_ref, curv_ref, vel_ref):
    wide = inv_ref.shape[1]

    def keep_phase(x, tile):
        curv_ref[1, x] = tile

    def keep_vel(x, tile):
        vel_ref[1, x] = tile

    def put_phase(x, value):
        curv_ref[0, x] = value

    def put_vel(x, value):
        vel_ref[0, x] = value

    unpack(low_ref, high_ref, 2, keep_phase)
    unpack(low_ref, high_ref, 3, keep_vel)
    fill(planes[2], wide, put_phase)
    fill(planes[3], wide, put_vel)

    @pl.loop(DEEP - COEF, wide - DEEP + COEF, unroll=4)
    def _(x):
        for t in range(2):
            phase = curv_ref[t, x]
            curvature = 3.0 * phase * phase - 1.0
            inverse = 1.0 / (1.0 + diffuse_coef * 42.0 + curv_coef * 6.0 * curvature)
            inv_ref[t, x] = inverse if t == 0 else inverse * mask
            curv_ref[t, x] = curv_coef * curvature


def steps(first, last, planes, rows, size, body):
    count = (last - first) // planes

    def chunk(start, n):
        for y in range(*rows, size):
            stores = []
            for j in range(n):
                stores += body(start + j, y)
            for store in stores:
                store()

    @pl.loop(0, count)
    def _(i):
        chunk(first + i * planes, planes)

    if first + count * planes < last:
        chunk(first + count * planes, last - first - count * planes)


def writer(ref, index, value):
    def store():
        ref[index] = value

    return store


def apply_operator(u_ref, lap_ref, curv_ref, vel_ref, mask, first, last, put):
    tall = curv_ref.shape[2]
    lanes = lanes_of((CHUNK, LANES))
    mask = mask[:CHUNK]

    def lap_part(x, y):
        lap = laplacian(u_ref, x, y, CHUNK, lanes)
        lap[1] = lap[1] * mask
        return [writer(lap_ref, (t, x, pl.ds(PAD + y, CHUNK)), lap[t]) for t in range(2)]

    steps(first - 1, last + 1, PLANES, (0, tall), CHUNK, lap_part)

    def image_part(x, y):
        twice = laplacian(lap_ref, x, y, CHUNK, lanes)
        out = []
        mine, wide = pl.ds(y, CHUNK), pl.ds(PAD + y, CHUNK)
        for t in range(2):
            flow = vel_ref[t, x + 1, mine] * u_ref[t, x + 1, wide] - vel_ref[t, x - 1, mine] * u_ref[t, x - 1, wide]
            image = (u_ref[t, x, wide] + diffuse_coef * twice[t]) - (
                curv_ref[t, x, mine] * lap_ref[t, x, wide] + (0.5 * advect_coef) * flow
            )
            out.append(put(t, x, mine, image))
        return out

    low = first // 8 * 8
    steps(first, last, PLANES, (low, tall - low), CHUNK, image_part)


def extend_basis(k, source_ref, older_ref, u_ref, lap_ref, inv_ref, curv_ref, vel_ref, mask, first, last, keep):
    down, centre, up = recurrence(k)
    tall = curv_ref.shape[2]

    def scale(x, y):
        mine = pl.ds(y, CHUNK)
        return [
            writer(u_ref, (t, x, pl.ds(PAD + y, CHUNK)), inv_ref[t, x, mine] * source_ref[t, x, mine]) for t in range(2)
        ]

    steps(first - 2, last + 2, PLANES, (0, tall), CHUNK, scale)

    def put(t, x, mine, image):
        fresh = (image - centre * source_ref[t, x, mine]) * (1.0 / up)
        if down:
            fresh = fresh - older_ref[t, x, mine]
        return writer(older_ref, (t, x, mine), fresh)

    apply_operator(u_ref, lap_ref, curv_ref, vel_ref, mask, first, last, put)
    blocks, rows = keep.shape[0], keep.shape[1]
    keep[...] = older_ref[0, DEEP : DEEP + blocks, DEEP : DEEP + rows, :]


def first_half_kernel(edge_ref, *refs):
    owns, halos, (low_ref, high_ref, basis_ref), rest = refs[:4], refs[4:12], refs[12:15], refs[15:]
    a_ref, b_ref, u_ref, lap_ref, inv_ref, curv_ref, vel_ref = rest
    wide, tall = inv_ref.shape[1], inv_ref.shape[2]
    blocks, rows = basis_ref.shape[1], basis_ref.shape[2]
    mask = inside_mask(edge_ref, tall)
    planes = planes_of(owns, halos)
    build_coefficients(planes, low_ref, high_ref, mask, inv_ref, curv_ref, vel_ref)

    def keep_start(x, tile):
        u_ref[1, x, PAD : PAD + tall] = tile * mask

    def keep_source(x, tile):
        a_ref[1, x] = tile

    def put_start(x, value):
        u_ref[0, x, PAD : PAD + tall] = value

    def put_source(x, value):
        a_ref[0, x] = value

    unpack(low_ref, high_ref, 0, keep_start)
    unpack(low_ref, high_ref, 1, keep_source)
    fill(planes[0], wide, put_start)
    fill(planes[1], wide, put_source)

    def put(t, x, mine, image):
        return writer(a_ref, (t, x, mine), a_ref[t, x, mine] - image)

    apply_operator(u_ref, lap_ref, curv_ref, vel_ref, mask, 2, wide - 2, put)
    basis_ref[0] = a_ref[0, DEEP : DEEP + blocks, DEEP : DEEP + rows, :]
    here, there = a_ref, b_ref
    for k in range(RESTART):
        margin = 2 * (k + 2)
        extend_basis(
            k, here, there, u_ref, lap_ref, inv_ref, curv_ref, vel_ref, mask, margin, wide - margin, basis_ref.at[k + 1]
        )
        here, there = there, here


def middle_pack_kernel(own, xlow, xhigh, ylow, yhigh, to_high, to_low):
    pack_ends([x_first(COEF, 0, 0, own, xlow, xhigh, ylow, yhigh)], to_high, to_low)


def second_half_kernel(edge_ref, *refs):
    owns, halos, (low_ref, high_ref), middle, rest = refs[:4], refs[4:12], refs[12:14], refs[14:21], refs[21:]
    own, xlow, xhigh, ylow, yhigh, qlow_ref, qhigh_ref = middle
    older_ref, basis_ref, sums_ref, a_ref, b_ref, u_ref, lap_ref, inv_ref, curv_ref, vel_ref = rest
    wide, tall = inv_ref.shape[1], inv_ref.shape[2]
    blocks, rows = older_ref.shape[1], older_ref.shape[2]
    mask = inside_mask(edge_ref, tall)
    build_coefficients(planes_of(owns, halos), low_ref, high_ref, mask, inv_ref, curv_ref, vel_ref)

    def keep(x, tile):
        a_ref[1, x] = tile

    def put_middle(x, value):
        a_ref[0, x] = value

    unpack(qlow_ref, qhigh_ref, 0, keep)
    fill(x_first(COEF, 0, 0, own, xlow, xhigh, ylow, yhigh), wide, put_middle)
    here, there = a_ref, b_ref
    for k in range(RESTART, STEPS):
        margin = DEEP - COEF + 2 * (k - RESTART + 1)
        extend_basis(
            k, here, there, u_ref, lap_ref, inv_ref, curv_ref, vel_ref, mask, margin, wide - margin, basis_ref.at[k - RESTART]
        )
        here, there = there, here

    def body(x, sums):
        planes = [older_ref[k, x] for k in range(RESTART + 1)] + [basis_ref[k, x] for k in range(STEPS - RESTART)]
        out = []
        for total, (i, j) in zip(sums, PAIRS):
            out.append(total + jnp.sum((planes[i] * planes[j]).reshape(rows // 8, 8, LANES), axis=0))
        return tuple(out)

    sums = lax.fori_loop(0, blocks, body, tuple(jnp.zeros((8, LANES), jnp.float32) for _ in PAIRS))
    lanes = lanes_of((8, LANES))
    packed = jnp.zeros((8, LANES), jnp.float32)
    for n, total in enumerate(sums):
        packed = jnp.where(lanes == n, jnp.sum(total, axis=1, keepdims=True), packed)
    packed = jnp.sum(packed, axis=0, keepdims=True)
    sums_ref[...] = jnp.broadcast_to(packed, sums_ref.shape)


def combine_kernel(parts_ref, older_ref, newer_ref, start_ref, phase_ref, adjoint_ref, residual_ref, sound_ref):
    blocks, rows = start_ref.shape[0], start_ref.shape[1]
    totals = jnp.sum(parts_ref[...].reshape(-1, 8, LANES), axis=0)
    totals = jnp.broadcast_to(jnp.sum(totals, axis=0, keepdims=True), (8, LANES))
    lanes = lanes_of((8, LANES))
    values = {
        pair: jnp.broadcast_to(jnp.sum(jnp.where(lanes == n, totals, 0.0), axis=1, keepdims=True), (8, LANES))
        for n, pair in enumerate(PAIRS)
    }
    gain, tail, sound = coefficients(lambda i, j: values[i, j])
    sound_ref[0] = jnp.min(sound)

    @pl.loop(0, blocks)
    def _(x):
        first, second = None, None
        for k in range(STEPS + 1):
            plane = (older_ref[k, x] if k <= RESTART else newer_ref[k - RESTART - 1, x]).reshape(rows // 8, 8, LANES)
            if gain[k] is not None:
                first = gain[k] * plane if first is None else first + gain[k] * plane
            second = tail[k] * plane if second is None else second + tail[k] * plane
        phase = phase_ref[x]
        curvature = 3.0 * phase * phase - 1.0
        inverse = 1.0 / (1.0 + diffuse_coef * 42.0 + curv_coef * 6.0 * curvature)
        adjoint_ref[x] = start_ref[x] + inverse * first.reshape(rows, LANES)
        residual_ref[x] = second.reshape(rows, LANES)


VMEM = pl.BlockSpec(memory_space=pltpu.VMEM)
SMEM = pl.BlockSpec(memory_space=pltpu.SMEM)


def call(kernel, outs, *args, scratch=(), scalars=0, flags=0):
    return pl.pallas_call(
        kernel,
        out_shape=[jax.ShapeDtypeStruct(shape, jnp.float32) for shape in outs],
        in_specs=[SMEM] * scalars + [VMEM] * (len(args) - scalars),
        out_specs=[VMEM] * (len(outs) - flags) + [SMEM] * flags,
        scratch_shapes=[pltpu.VMEM(shape, jnp.float32) for shape in scratch],
        compiler_params=pltpu.CompilerParams(vmem_limit_bytes=32 * 2**20),
    )(*args)


def swapped(to_high, to_low, axis, wrap):
    peers = lax.axis_size(axis)
    up = [(i, (i + 1) % peers) for i in range(peers if wrap else peers - 1)]
    return lax.ppermute(to_high, axis, up), lax.ppermute(to_low, axis, [(j, i) for i, j in up])


def on_device(adjoint_source, start_guess, phase, velocity):
    blocks, rows, _ = phase.shape
    wide, tall = blocks + 2 * DEEP, rows + 2 * DEEP
    place = lax.axis_index("gz")
    edge = jnp.where(place == 0, 1, jnp.where(place == lax.axis_size("gz") - 1, 2, 0)).astype(jnp.int32).reshape(1)
    scratch = [(2, wide, tall + 2 * PAD * (2 <= n < 4), LANES) for n in range(7)]
    owns = [start_guess, adjoint_source, phase, velocity]

    xa, xb = sum(PARTS[:2]), sum(PARTS[2:])
    outs = ((xa, rows, LANES),) * 2 + ((2 * blocks, DEEP, LANES),) * 2
    xa_high, xa_low, yb_high, yb_low = call(start_kernel, outs, *owns)
    yb = swapped(yb_high, yb_low, "gy", True)
    halos = [*swapped(xa_high, xa_low, "gx", True), *yb]
    outs = ((2 * (blocks + xa), DEEP, LANES),) * 2 + ((xb, tall, LANES),) * 2
    ya_high, ya_low, xb_high, xb_low = call(turn_kernel, outs, *owns, *halos)
    halos += [*swapped(ya_high, ya_low, "gy", True), *swapped(xb_high, xb_low, "gx", True)]

    def pack(*refs):
        pack_ends(planes_of(refs[:4], refs[4:12]), *refs[12:])

    ends = swapped(*call(pack, ((4, wide // GROUP, tall, LANES),) * 2, *owns, *halos), "gz", False)
    known = [edge, *owns, *halos, *ends]
    (older,) = call(first_half_kernel, ((RESTART + 1, blocks, rows, LANES),), *known, scratch=scratch, scalars=1)

    middle = older[RESTART]
    xq = swapped(middle[blocks - COEF :], middle[:COEF], "gx", True)

    def pack_middle(own, low, high, to_high, to_low):
        pack_rows([COEF], [own], low, high, to_high, to_low)

    yq = swapped(*call(pack_middle, ((blocks + 2 * COEF, DEEP, LANES),) * 2, middle, *xq), "gy", True)
    zq = swapped(*call(middle_pack_kernel, ((1, wide // GROUP, tall, LANES),) * 2, middle, *xq, *yq), "gz", False)
    newer, sums = call(
        second_half_kernel,
        ((STEPS - RESTART, blocks, rows, LANES), (lax.axis_size(AXES), LANES)),
        *known, middle, *xq, *yq, *zq, older, scratch=scratch, scalars=1,
    )
    parts = lax.all_to_all(sums, AXES, 0, 0, tiled=True)
    adjoint, residual, sound = call(
        combine_kernel, (phase.shape, phase.shape, (1,)), parts, older, newer, start_guess, phase, flags=1
    )

    def plain(state):
        return (jnp.float32(1.0), *plain_solve(adjoint_source, start_guess, phase, velocity))

    return lax.while_loop(lambda state: ~(state[0] > 0.5), plain, (sound[0], adjoint, residual))[1:]


def solution(mesh):
    placed = P("gx", "gy", "gz")
    return jax.shard_map(on_device, mesh=mesh, in_specs=(placed,) * 4, out_specs=(placed,) * 2, check_vma=False)
```

```python
import functools

import jax
import jax.numpy as jnp
from jax import lax
from jax.experimental import pallas as pl
from jax.experimental.pallas import tpu as pltpu
from jax.sharding import PartitionSpec as P

ITERS = 3
STEPS = 2 * ITERS
RESTART = 3
CENTRE = 1.3
RADIUS = 1.3
KAPPA_MAX = 4000.0
AXES = ("gx", "gy", "gz")
PAIRS = [(i, j) for i in range(STEPS + 1) for j in range(i, STEPS + 1)]
DEEP = 8
COEF = 6
LANES = 128
PAD = 8
CHUNK = 8
PLANES = 16
PARTS = (DEEP, COEF, COEF, COEF + 1)
GROUP = LANES // DEEP

diffuse_coef = 0.05
curv_coef = 0.2
advect_coef = 0.25


def extended(value, sides, width):
    for axis, dim in sides:
        peers, length = (lax.axis_size(axis), value.shape[dim])
        up = [(i, (i + 1) % peers) for i in range(peers)]
        down = [(j, i) for i, j in up]
        last = lax.slice_in_dim(value, length - width, length, axis=dim)
        first = lax.slice_in_dim(value, 0, width, axis=dim)
        before = lax.ppermute(last, axis, up)
        after = lax.ppermute(first, axis, down)
        value = jnp.concatenate([before, value, after], axis=dim)
    return value


def wall_mask(width, depth):
    planes = jnp.arange(depth + 2 * width, dtype=jnp.int32)
    global_z = lax.axis_index("gz") * depth + planes - width
    inside = (global_z >= 0) & (global_z < depth * lax.axis_size("gz"))
    return inside.astype(jnp.float32)


def lap_inner(padded):
    total = padded[2:, 1:-1, 1:-1] + padded[:-2, 1:-1, 1:-1]
    total = total + padded[1:-1, 2:, 1:-1] + padded[1:-1, :-2, 1:-1]
    total = total + padded[1:-1, 1:-1, 2:] + padded[1:-1, 1:-1, :-2]
    return total - 6.0 * padded[1:-1, 1:-1, 1:-1]


def operate(field, curvature, vel_rims):
    depth = field.shape[2]
    padded = extended(field, (("gx", 0), ("gy", 1), ("gz", 2)), 2)
    padded = padded * wall_mask(2, depth)
    lap_wide = lap_inner(padded) * wall_mask(1, depth)
    lap_two = lap_inner(lap_wide)
    lap_one = lap_wide[1:-1, 1:-1, 1:-1]
    ahead = padded[3:-1, 2:-2, 2:-2]
    behind = padded[1:-3, 2:-2, 2:-2]
    advect = 0.5 * (vel_rims[2:] * ahead - vel_rims[:-2] * behind)
    return field + diffuse_coef * lap_two - curv_coef * curvature * lap_one - advect_coef * advect


def plain_solve(adjoint_source, start_guess, phase, velocity):
    vel_rims = extended(velocity, (("gx", 0),), 1)
    curvature = 3.0 * phase * phase - 1.0
    inverse_diag = 1.0 / (1.0 + diffuse_coef * 42.0 + curv_coef * 6.0 * curvature)
    adjoint = start_guess
    residual = adjoint_source - operate(adjoint, curvature, vel_rims)
    shadow = residual
    search = residual
    shadow_dot = lax.psum(jnp.sum(shadow * residual), AXES)
    for step in range(ITERS):
        search_hat = inverse_diag * search
        image = operate(search_hat, curvature, vel_rims)
        step_len = shadow_dot / lax.psum(jnp.sum(shadow * image), AXES)
        middle = residual - step_len * image
        middle_hat = inverse_diag * middle
        second = operate(middle_hat, curvature, vel_rims)
        cross, square = lax.psum((jnp.sum(second * middle), jnp.sum(second * second)), AXES)
        stabil = cross / square
        adjoint = adjoint + step_len * search_hat + stabil * middle_hat
        residual = middle - stabil * second
        if step + 1 < ITERS:
            new_dot = lax.psum(jnp.sum(shadow * residual), AXES)
            blend = new_dot / shadow_dot * (step_len / stabil)
            search = residual + blend * (search - stabil * image)
            shadow_dot = new_dot
    return adjoint, residual


def recurrence(k):
    if k % RESTART == 0:
        return 0.0, CENTRE, RADIUS
    return 0.5 * RADIUS, CENTRE, 0.5 * RADIUS


def coefficients(gram):
    def add(*terms):
        total = None
        for factor, value in terms:
            if value is None:
                continue
            piece = value if factor is None else factor * value
            total = piece if total is None else total + piece
        return total

    def apply(vec):
        out = [None] * (STEPS + 1)
        for k in range(STEPS):
            if vec[k] is None:
                continue
            for shift, weight in zip((-1, 0, 1), recurrence(k)):
                if weight:
                    out[k + shift] = add((None, out[k + shift]), (weight, vec[k]))
        return out

    one = jnp.ones_like(gram(0, 0))
    kappa = [one]

    def dot(a, b):
        total, size = None, None
        for j in range(STEPS + 1):
            if b[j] is None:
                continue
            row, row_size = None, None
            for i in range(STEPS + 1):
                if a[i] is None:
                    continue
                piece = a[i] * gram(min(i, j), max(i, j))
                row = piece if row is None else row + piece
                row_size = jnp.abs(piece) if row_size is None else row_size + jnp.abs(piece)
            total = add((None, total), (b[j], row))
            size = add((None, size), (jnp.abs(b[j]), row_size))
        kappa[0] = jnp.where(size <= KAPPA_MAX * jnp.abs(total), kappa[0], 0.0)
        return total

    def combine(*terms):
        return [add(*((factor, vec[k]) for factor, vec in terms)) for k in range(STEPS + 1)]

    unit = [one] + [None] * STEPS
    residual, search, shadow = unit, unit, unit
    gain = [None] * (STEPS + 1)
    shadow_dot = dot(shadow, residual)
    for step in range(ITERS):
        image = apply(search)
        step_len = shadow_dot / dot(shadow, image)
        middle = combine((None, residual), (-step_len, image))
        second = apply(middle)
        stabil = dot(second, middle) / dot(second, second)
        gain = combine((None, gain), (step_len, search), (stabil, middle))
        residual = combine((None, middle), (-stabil, second))
        if step + 1 < ITERS:
            new_dot = dot(shadow, residual)
            blend = new_dot / shadow_dot * (step_len / stabil)
            search = combine((None, residual), (blend, search), (-blend * stabil, image))
            shadow_dot = new_dot
    dot(residual, residual)
    return gain, residual, kappa[0]


def lanes_of(shape):
    return lax.broadcasted_iota(jnp.int32, shape, len(shape) - 1)


def x_first(depth, start, at, own, xlow, xhigh, ylow, yhigh):
    blocks, gap = own.shape[0], DEEP - depth

    def plane(x):
        n = x - gap
        if not 0 <= n < blocks + 2 * depth:
            return None
        if n < depth:
            middle = xlow[start + n]
        elif n < depth + blocks:
            middle = own[n - depth]
        else:
            middle = xhigh[start + n - depth - blocks]
        return jnp.concatenate([ylow[at + n], middle, yhigh[at + n]], axis=0)

    return plane


def y_first(depth, start, at, own, xlow, xhigh, ylow, yhigh):
    blocks, gap = own.shape[0], DEEP - depth

    def plane(x):
        n = x - gap
        if not 0 <= n < blocks + 2 * depth:
            return None
        if n < depth:
            return xlow[start + n]
        if n >= depth + blocks:
            return xhigh[start + n - depth - blocks]
        m = n - depth
        return jnp.concatenate([ylow[at + m], own[m], yhigh[at + m]], axis=0)

    return plane


def pack_rows(parts, owns, low, high, to_high, to_low):
    start, at = 0, 0
    for depth, own in zip(parts, owns):
        blocks, rows = own.shape[0], own.shape[1]
        for first, ref, size in ((start, low, depth), (0, own, blocks), (start, high, depth)):
            to_high[at : at + size] = ref[first : first + size, rows - DEEP :, :]
            to_low[at : at + size] = ref[first : first + size, :DEEP, :]
            at += size
        start += depth


def pack_planes(parts, owns, low, high, to_high, to_low):
    start, at = 0, 0
    for depth, own in zip(parts, owns):
        blocks = own.shape[0]
        for n in range(depth):
            for first, ref in ((0, to_low), (blocks - depth, to_high)):
                m = first + n
                ref[start + n] = jnp.concatenate([low[at + m], own[m], high[at + m]], axis=0)
        start += depth
        at += blocks


def pack_ends(planes, to_high, to_low):
    groups, tall = to_high.shape[1], to_high.shape[2]
    lanes = lanes_of((tall, LANES))
    for a, plane in enumerate(planes):
        for g in range(groups):
            up = jnp.zeros((tall, LANES), jnp.float32)
            down = jnp.zeros((tall, LANES), jnp.float32)
            for i in range(GROUP):
                value = plane(g * GROUP + i)
                if value is None:
                    continue
                value = turn(value, DEEP * (i + 1))
                up = jnp.where(lanes // DEEP == i, value, up)
                down = jnp.where(lanes // DEEP == (i + 1) % GROUP, value, down)
            to_high[a, g] = up
            to_low[a, g] = down


def start_kernel(one, two, three, four, xa_high, xa_low, yb_high, yb_low):
    blocks, rows = one.shape[0], one.shape[1]
    at = 0
    for depth, own in zip(PARTS[:2], (one, two)):
        xa_high[at : at + depth] = own[blocks - depth :]
        xa_low[at : at + depth] = own[:depth]
        at += depth
    for n, own in enumerate((three, four)):
        yb_high[n * blocks : (n + 1) * blocks] = own[:, rows - DEEP :, :]
        yb_low[n * blocks : (n + 1) * blocks] = own[:, :DEEP, :]


def turn_kernel(one, two, three, four, xalow, xahigh, yblow, ybhigh, ya_high, ya_low, xb_high, xb_low):
    pack_rows(PARTS[:2], (one, two), xalow, xahigh, ya_high, ya_low)
    pack_planes(PARTS[2:], (three, four), yblow, ybhigh, xb_high, xb_low)


def planes_of(owns, halos):
    xalow, xahigh, yblow, ybhigh, yalow, yahigh, xblow, xbhigh = halos
    blocks = owns[0].shape[0]
    first = [
        x_first(PARTS[0], 0, 0, owns[0], xalow, xahigh, yalow, yahigh),
        x_first(PARTS[1], PARTS[0], blocks + 2 * PARTS[0], owns[1], xalow, xahigh, yalow, yahigh),
    ]
    return first + [
        y_first(PARTS[2], 0, 0, owns[2], xblow, xbhigh, yblow, ybhigh),
        y_first(PARTS[3], PARTS[2], blocks, owns[3], xblow, xbhigh, yblow, ybhigh),
    ]


def fill(plane, count, put):
    for x in range(count):
        value = plane(x)
        if value is not None:
            put(x, value)


def turn(plane, shift, axis=1):
    shift = shift % plane.shape[axis]
    return pltpu.roll(plane, shift, axis) if shift else plane


def unpack(low_ref, high_ref, a, put):
    groups, tall = low_ref.shape[1], low_ref.shape[2]
    lanes = lanes_of((tall, LANES))
    outer = jnp.logical_or(lanes < DEEP, lanes >= LANES - DEEP)
    for g in range(groups):
        below, above = low_ref[a, g], high_ref[a, g]
        for i in range(GROUP):
            tile = turn(jnp.where(lanes // DEEP == i, below, above), -DEEP * (i + 1))
            put(g * GROUP + i, jnp.where(outer, tile, 0.0))


def inside_mask(edge_ref, tall):
    lanes = lanes_of((tall, LANES))
    edge = edge_ref[0]
    above = jnp.logical_and(lanes < DEEP, edge != 2)
    below = jnp.logical_and(lanes >= LANES - DEEP, edge != 1)
    return jnp.where(jnp.logical_or(above, below), 1.0, 0.0)


def laplacian(ref, x, y, size, lanes):
    here = pl.ds(PAD + y, size)
    mid = [ref[t, x, here, :] for t in range(2)]
    ahead = [turn(m, -1) for m in mid]
    behind = [turn(m, 1) for m in mid]
    out = []
    for t in range(2):
        along = jnp.where(lanes == LANES - 1, ahead[1 - t], ahead[t]) + jnp.where(lanes == 0, behind[1 - t], behind[t])
        across = ref[t, x, pl.ds(PAD + y - 1, size), :] + ref[t, x, pl.ds(PAD + y + 1, size), :]
        out.append((ref[t, x - 1, here, :] + ref[t, x + 1, here, :]) + (across + along) - 6.0 * mid[t])
    return out


def build_coefficients(planes, low_ref, high_ref, mask, inv_ref, curv_ref, vel_ref):
    wide = inv_ref.shape[1]

    def keep_phase(x, tile):
        curv_ref[1, x] = tile

    def keep_vel(x, tile):
        vel_ref[1, x] = tile

    def put_phase(x, value):
        curv_ref[0, x] = value

    def put_vel(x, value):
        vel_ref[0, x] = value

    unpack(low_ref, high_ref, 2, keep_phase)
    unpack(low_ref, high_ref, 3, keep_vel)
    fill(planes[2], wide, put_phase)
    fill(planes[3], wide, put_vel)

    @pl.loop(DEEP - COEF, wide - DEEP + COEF, unroll=4)
    def _(x):
        for t in range(2):
            phase = curv_ref[t, x]
            curvature = 3.0 * phase * phase - 1.0
            inverse = 1.0 / (1.0 + diffuse_coef * 42.0 + curv_coef * 6.0 * curvature)
            inv_ref[t, x] = inverse if t == 0 else inverse * mask
            curv_ref[t, x] = curv_coef * curvature


def steps(first, last, planes, rows, size, body):
    count = (last - first) // planes

    def chunk(start, n):
        for y in range(*rows, size):
            stores = []
            for j in range(n):
                stores += body(start + j, y)
            for store in stores:
                store()

    @pl.loop(0, count)
    def _(i):
        chunk(first + i * planes, planes)

    if first + count * planes < last:
        chunk(first + count * planes, last - first - count * planes)


def writer(ref, index, value):
    def store():
        ref[index] = value

    return store


def apply_operator(u_ref, lap_ref, curv_ref, vel_ref, mask, first, last, put):
    tall = curv_ref.shape[2]
    lanes = lanes_of((CHUNK, LANES))
    mask = mask[:CHUNK]

    def lap_part(x, y):
        lap = laplacian(u_ref, x, y, CHUNK, lanes)
        lap[1] = lap[1] * mask
        return [writer(lap_ref, (t, x, pl.ds(PAD + y, CHUNK)), lap[t]) for t in range(2)]

    steps(first - 1, last + 1, PLANES, (0, tall), CHUNK, lap_part)

    def image_part(x, y):
        twice = laplacian(lap_ref, x, y, CHUNK, lanes)
        out = []
        mine, wide = pl.ds(y, CHUNK), pl.ds(PAD + y, CHUNK)
        for t in range(2):
            flow = vel_ref[t, x + 1, mine] * u_ref[t, x + 1, wide] - vel_ref[t, x - 1, mine] * u_ref[t, x - 1, wide]
            image = (u_ref[t, x, wide] + diffuse_coef * twice[t]) - (
                curv_ref[t, x, mine] * lap_ref[t, x, wide] + (0.5 * advect_coef) * flow
            )
            out += put(t, x, mine, image)
        return out

    low = first // 8 * 8
    steps(first, last, PLANES, (low, tall - low), CHUNK, image_part)


def scaled(next_ref, inv_ref, t, x, mine, value):
    return writer(next_ref, (t, x, pl.ds(PAD + mine.start, CHUNK)), inv_ref[t, x, mine] * value)


def extend_basis(k, source_ref, older_ref, u_ref, next_ref, lap_ref, inv_ref, curv_ref, vel_ref, mask, margin, keep):
    down, centre, up = recurrence(k)
    wide = inv_ref.shape[1]

    def put(t, x, mine, image):
        fresh = (image - centre * source_ref[t, x, mine]) * (1.0 / up)
        if down:
            fresh = fresh - older_ref[t, x, mine]
        stores = [writer(older_ref, (t, x, mine), fresh)]
        if (k + 1) % RESTART:
            stores.append(scaled(next_ref, inv_ref, t, x, mine, fresh))
        return stores

    apply_operator(u_ref, lap_ref, curv_ref, vel_ref, mask, margin, wide - margin, put)
    blocks, rows = keep.shape[0], keep.shape[1]
    keep[...] = older_ref[0, DEEP : DEEP + blocks, DEEP : DEEP + rows, :]


def first_half_kernel(edge_ref, *refs):
    owns, halos, (low_ref, high_ref, basis_ref), rest = refs[:4], refs[4:12], refs[12:15], refs[15:]
    a_ref, b_ref, u_ref, v_ref, lap_ref, inv_ref, curv_ref, vel_ref = rest
    wide, tall = inv_ref.shape[1], inv_ref.shape[2]
    blocks, rows = basis_ref.shape[1], basis_ref.shape[2]
    mask = inside_mask(edge_ref, tall)
    planes = planes_of(owns, halos)
    build_coefficients(planes, low_ref, high_ref, mask, inv_ref, curv_ref, vel_ref)

    def keep_start(x, tile):
        u_ref[1, x, PAD : PAD + tall] = tile * mask

    def keep_source(x, tile):
        a_ref[1, x] = tile

    def put_start(x, value):
        u_ref[0, x, PAD : PAD + tall] = value

    def put_source(x, value):
        a_ref[0, x] = value

    unpack(low_ref, high_ref, 0, keep_start)
    unpack(low_ref, high_ref, 1, keep_source)
    fill(planes[0], wide, put_start)
    fill(planes[1], wide, put_source)

    def put(t, x, mine, image):
        first = a_ref[t, x, mine] - image
        return [writer(a_ref, (t, x, mine), first), scaled(v_ref, inv_ref, t, x, mine, first)]

    apply_operator(u_ref, lap_ref, curv_ref, vel_ref, mask, 2, wide - 2, put)
    basis_ref[0] = a_ref[0, DEEP : DEEP + blocks, DEEP : DEEP + rows, :]
    here, there, now, later = a_ref, b_ref, v_ref, u_ref
    for k in range(RESTART):
        extend_basis(
            k, here, there, now, later, lap_ref, inv_ref, curv_ref, vel_ref, mask, 2 * (k + 2), basis_ref.at[k + 1]
        )
        here, there, now, later = there, here, later, now


def middle_pack_kernel(own, xlow, xhigh, ylow, yhigh, to_high, to_low):
    pack_ends([x_first(COEF, 0, 0, own, xlow, xhigh, ylow, yhigh)], to_high, to_low)


def second_half_kernel(edge_ref, *refs):
    owns, halos, (low_ref, high_ref), middle, rest = refs[:4], refs[4:12], refs[12:14], refs[14:21], refs[21:]
    own, xlow, xhigh, ylow, yhigh, qlow_ref, qhigh_ref = middle
    older_ref, basis_ref, sums_ref, a_ref, b_ref, u_ref, v_ref, lap_ref, inv_ref, curv_ref, vel_ref = rest
    wide, tall = inv_ref.shape[1], inv_ref.shape[2]
    blocks, rows = older_ref.shape[1], older_ref.shape[2]
    mask = inside_mask(edge_ref, tall)
    build_coefficients(planes_of(owns, halos), low_ref, high_ref, mask, inv_ref, curv_ref, vel_ref)

    def keep(x, tile):
        a_ref[1, x] = tile

    def put_middle(x, value):
        a_ref[0, x] = value

    unpack(qlow_ref, qhigh_ref, 0, keep)
    fill(x_first(COEF, 0, 0, own, xlow, xhigh, ylow, yhigh), wide, put_middle)

    def scale(x, y):
        return [scaled(u_ref, inv_ref, t, x, pl.ds(y, CHUNK), a_ref[t, x, pl.ds(y, CHUNK)]) for t in range(2)]

    steps(DEEP - COEF, wide - DEEP + COEF, PLANES, (0, tall), CHUNK, scale)
    here, there, now, later = a_ref, b_ref, u_ref, v_ref
    for k in range(RESTART, STEPS):
        n = k - RESTART
        extend_basis(
            k, here, there, now, later, lap_ref, inv_ref, curv_ref, vel_ref, mask, DEEP - COEF + 2 * (n + 1), basis_ref.at[n]
        )
        here, there, now, later = there, here, later, now

    def body(x, sums):
        planes = [older_ref[k, x] for k in range(RESTART + 1)] + [basis_ref[k, x] for k in range(STEPS - RESTART)]
        out = []
        for total, (i, j) in zip(sums, PAIRS):
            out.append(total + jnp.sum((planes[i] * planes[j]).reshape(rows // 8, 8, LANES), axis=0))
        return tuple(out)

    sums = lax.fori_loop(0, blocks, body, tuple(jnp.zeros((8, LANES), jnp.float32) for _ in PAIRS))
    lanes = lanes_of((8, LANES))
    packed = jnp.zeros((8, LANES), jnp.float32)
    for n, total in enumerate(sums):
        packed = jnp.where(lanes == n, jnp.sum(total, axis=1, keepdims=True), packed)
    packed = jnp.sum(packed, axis=0, keepdims=True)
    sums_ref[...] = jnp.broadcast_to(packed, sums_ref.shape)


def combine_kernel(parts_ref, older_ref, newer_ref, start_ref, phase_ref, adjoint_ref, residual_ref, sound_ref):
    blocks, rows = start_ref.shape[0], start_ref.shape[1]
    totals = jnp.sum(parts_ref[...].reshape(-1, 8, LANES), axis=0)
    totals = jnp.broadcast_to(jnp.sum(totals, axis=0, keepdims=True), (8, LANES))
    lanes = lanes_of((8, LANES))
    values = {
        pair: jnp.broadcast_to(jnp.sum(jnp.where(lanes == n, totals, 0.0), axis=1, keepdims=True), (8, LANES))
        for n, pair in enumerate(PAIRS)
    }
    gain, tail, sound = coefficients(lambda i, j: values[i, j])
    sound_ref[0] = jnp.min(sound)

    @pl.loop(0, blocks)
    def _(x):
        first, second = None, None
        for k in range(STEPS + 1):
            plane = (older_ref[k, x] if k <= RESTART else newer_ref[k - RESTART - 1, x]).reshape(rows // 8, 8, LANES)
            if gain[k] is not None:
                first = gain[k] * plane if first is None else first + gain[k] * plane
            second = tail[k] * plane if second is None else second + tail[k] * plane
        phase = phase_ref[x]
        curvature = 3.0 * phase * phase - 1.0
        inverse = 1.0 / (1.0 + diffuse_coef * 42.0 + curv_coef * 6.0 * curvature)
        adjoint_ref[x] = start_ref[x] + inverse * first.reshape(rows, LANES)
        residual_ref[x] = second.reshape(rows, LANES)


VMEM = pl.BlockSpec(memory_space=pltpu.VMEM)
SMEM = pl.BlockSpec(memory_space=pltpu.SMEM)


def call(kernel, outs, *args, scratch=(), scalars=0, flags=0):
    return pl.pallas_call(
        kernel,
        out_shape=[jax.ShapeDtypeStruct(shape, jnp.float32) for shape in outs],
        in_specs=[SMEM] * scalars + [VMEM] * (len(args) - scalars),
        out_specs=[VMEM] * (len(outs) - flags) + [SMEM] * flags,
        scratch_shapes=[pltpu.VMEM(shape, jnp.float32) for shape in scratch],
        compiler_params=pltpu.CompilerParams(vmem_limit_bytes=32 * 2**20),
    )(*args)


def swapped(to_high, to_low, axis, wrap):
    peers = lax.axis_size(axis)
    up = [(i, (i + 1) % peers) for i in range(peers if wrap else peers - 1)]
    return lax.ppermute(to_high, axis, up), lax.ppermute(to_low, axis, [(j, i) for i, j in up])


def on_device(adjoint_source, start_guess, phase, velocity):
    blocks, rows, _ = phase.shape
    wide, tall = blocks + 2 * DEEP, rows + 2 * DEEP
    place = lax.axis_index("gz")
    edge = jnp.where(place == 0, 1, jnp.where(place == lax.axis_size("gz") - 1, 2, 0)).astype(jnp.int32).reshape(1)
    scratch = [(2, wide, tall + 2 * PAD * (2 <= n < 5), LANES) for n in range(8)]
    owns = [start_guess, adjoint_source, phase, velocity]

    xa, xb = sum(PARTS[:2]), sum(PARTS[2:])
    outs = ((xa, rows, LANES),) * 2 + ((2 * blocks, DEEP, LANES),) * 2
    xa_high, xa_low, yb_high, yb_low = call(start_kernel, outs, *owns)
    yb = swapped(yb_high, yb_low, "gy", True)
    halos = [*swapped(xa_high, xa_low, "gx", True), *yb]
    outs = ((2 * (blocks + xa), DEEP, LANES),) * 2 + ((xb, tall, LANES),) * 2
    ya_high, ya_low, xb_high, xb_low = call(turn_kernel, outs, *owns, *halos)
    halos += [*swapped(ya_high, ya_low, "gy", True), *swapped(xb_high, xb_low, "gx", True)]

    def pack(*refs):
        pack_ends(planes_of(refs[:4], refs[4:12]), *refs[12:])

    ends = swapped(*call(pack, ((4, wide // GROUP, tall, LANES),) * 2, *owns, *halos), "gz", False)
    known = [edge, *owns, *halos, *ends]
    (older,) = call(first_half_kernel, ((RESTART + 1, blocks, rows, LANES),), *known, scratch=scratch, scalars=1)

    middle = older[RESTART]
    xq = swapped(middle[blocks - COEF :], middle[:COEF], "gx", True)

    def pack_middle(own, low, high, to_high, to_low):
        pack_rows([COEF], [own], low, high, to_high, to_low)

    yq = swapped(*call(pack_middle, ((blocks + 2 * COEF, DEEP, LANES),) * 2, middle, *xq), "gy", True)
    zq = swapped(*call(middle_pack_kernel, ((1, wide // GROUP, tall, LANES),) * 2, middle, *xq, *yq), "gz", False)
    newer, sums = call(
        second_half_kernel,
        ((STEPS - RESTART, blocks, rows, LANES), (lax.axis_size(AXES), LANES)),
        *known, middle, *xq, *yq, *zq, older, scratch=scratch, scalars=1,
    )
    parts = lax.all_to_all(sums, AXES, 0, 0, tiled=True)
    adjoint, residual, sound = call(
        combine_kernel, (phase.shape, phase.shape, (1,)), parts, older, newer, start_guess, phase, flags=1
    )

    def plain(state):
        return (jnp.float32(1.0), *plain_solve(adjoint_source, start_guess, phase, velocity))

    return lax.while_loop(lambda state: ~(state[0] > 0.5), plain, (sound[0], adjoint, residual))[1:]


def solution(mesh):
    placed = P("gx", "gy", "gz")
    return jax.shard_map(on_device, mesh=mesh, in_specs=(placed,) * 4, out_specs=(placed,) * 2, check_vma=False)
```

```python
import functools

import jax
import jax.numpy as jnp
from jax import lax
from jax.experimental import pallas as pl
from jax.experimental.pallas import tpu as pltpu
from jax.sharding import PartitionSpec as P

ITERS = 3
STEPS = 2 * ITERS
RESTART = 3
CENTRE = 1.3
RADIUS = 1.3
KAPPA_MAX = 4000.0
AXES = ("gx", "gy", "gz")
PAIRS = [(i, j) for i in range(STEPS + 1) for j in range(i, STEPS + 1)]
DEEP = 8
COEF = 6
LANES = 128
PAD = 8
CHUNK = 8
PLANES = 16
PARTS = (DEEP, COEF, COEF, COEF + 1)
GROUP = LANES // DEEP

diffuse_coef = 0.05
curv_coef = 0.2
advect_coef = 0.25


def extended(value, sides, width):
    for axis, dim in sides:
        peers, length = (lax.axis_size(axis), value.shape[dim])
        up = [(i, (i + 1) % peers) for i in range(peers)]
        down = [(j, i) for i, j in up]
        last = lax.slice_in_dim(value, length - width, length, axis=dim)
        first = lax.slice_in_dim(value, 0, width, axis=dim)
        before = lax.ppermute(last, axis, up)
        after = lax.ppermute(first, axis, down)
        value = jnp.concatenate([before, value, after], axis=dim)
    return value


def wall_mask(width, depth):
    planes = jnp.arange(depth + 2 * width, dtype=jnp.int32)
    global_z = lax.axis_index("gz") * depth + planes - width
    inside = (global_z >= 0) & (global_z < depth * lax.axis_size("gz"))
    return inside.astype(jnp.float32)


def lap_inner(padded):
    total = padded[2:, 1:-1, 1:-1] + padded[:-2, 1:-1, 1:-1]
    total = total + padded[1:-1, 2:, 1:-1] + padded[1:-1, :-2, 1:-1]
    total = total + padded[1:-1, 1:-1, 2:] + padded[1:-1, 1:-1, :-2]
    return total - 6.0 * padded[1:-1, 1:-1, 1:-1]


def operate(field, curvature, vel_rims):
    depth = field.shape[2]
    padded = extended(field, (("gx", 0), ("gy", 1), ("gz", 2)), 2)
    padded = padded * wall_mask(2, depth)
    lap_wide = lap_inner(padded) * wall_mask(1, depth)
    lap_two = lap_inner(lap_wide)
    lap_one = lap_wide[1:-1, 1:-1, 1:-1]
    ahead = padded[3:-1, 2:-2, 2:-2]
    behind = padded[1:-3, 2:-2, 2:-2]
    advect = 0.5 * (vel_rims[2:] * ahead - vel_rims[:-2] * behind)
    return field + diffuse_coef * lap_two - curv_coef * curvature * lap_one - advect_coef * advect


def plain_solve(adjoint_source, start_guess, phase, velocity):
    vel_rims = extended(velocity, (("gx", 0),), 1)
    curvature = 3.0 * phase * phase - 1.0
    inverse_diag = 1.0 / (1.0 + diffuse_coef * 42.0 + curv_coef * 6.0 * curvature)
    adjoint = start_guess
    residual = adjoint_source - operate(adjoint, curvature, vel_rims)
    shadow = residual
    search = residual
    shadow_dot = lax.psum(jnp.sum(shadow * residual), AXES)
    for step in range(ITERS):
        search_hat = inverse_diag * search
        image = operate(search_hat, curvature, vel_rims)
        step_len = shadow_dot / lax.psum(jnp.sum(shadow * image), AXES)
        middle = residual - step_len * image
        middle_hat = inverse_diag * middle
        second = operate(middle_hat, curvature, vel_rims)
        cross, square = lax.psum((jnp.sum(second * middle), jnp.sum(second * second)), AXES)
        stabil = cross / square
        adjoint = adjoint + step_len * search_hat + stabil * middle_hat
        residual = middle - stabil * second
        if step + 1 < ITERS:
            new_dot = lax.psum(jnp.sum(shadow * residual), AXES)
            blend = new_dot / shadow_dot * (step_len / stabil)
            search = residual + blend * (search - stabil * image)
            shadow_dot = new_dot
    return adjoint, residual


def recurrence(k):
    if k % RESTART == 0:
        return 0.0, CENTRE, RADIUS
    return 0.5 * RADIUS, CENTRE, 0.5 * RADIUS


def coefficients(gram):
    def add(*terms):
        total = None
        for factor, value in terms:
            if value is None:
                continue
            piece = value if factor is None else factor * value
            total = piece if total is None else total + piece
        return total

    def apply(vec):
        out = [None] * (STEPS + 1)
        for k in range(STEPS):
            if vec[k] is None:
                continue
            for shift, weight in zip((-1, 0, 1), recurrence(k)):
                if weight:
                    out[k + shift] = add((None, out[k + shift]), (weight, vec[k]))
        return out

    one = jnp.ones_like(gram(0, 0))
    kappa = [one]

    def dot(a, b):
        total, size = None, None
        for j in range(STEPS + 1):
            if b[j] is None:
                continue
            row, row_size = None, None
            for i in range(STEPS + 1):
                if a[i] is None:
                    continue
                piece = a[i] * gram(min(i, j), max(i, j))
                row = piece if row is None else row + piece
                row_size = jnp.abs(piece) if row_size is None else row_size + jnp.abs(piece)
            total = add((None, total), (b[j], row))
            size = add((None, size), (jnp.abs(b[j]), row_size))
        kappa[0] = jnp.where(size <= KAPPA_MAX * jnp.abs(total), kappa[0], 0.0)
        return total

    def combine(*terms):
        return [add(*((factor, vec[k]) for factor, vec in terms)) for k in range(STEPS + 1)]

    unit = [one] + [None] * STEPS
    residual, search, shadow = unit, unit, unit
    gain = [None] * (STEPS + 1)
    shadow_dot = dot(shadow, residual)
    for step in range(ITERS):
        image = apply(search)
        step_len = shadow_dot / dot(shadow, image)
        middle = combine((None, residual), (-step_len, image))
        second = apply(middle)
        stabil = dot(second, middle) / dot(second, second)
        gain = combine((None, gain), (step_len, search), (stabil, middle))
        residual = combine((None, middle), (-stabil, second))
        if step + 1 < ITERS:
            new_dot = dot(shadow, residual)
            blend = new_dot / shadow_dot * (step_len / stabil)
            search = combine((None, residual), (blend, search), (-blend * stabil, image))
            shadow_dot = new_dot
    dot(residual, residual)
    return gain, residual, kappa[0]


def lanes_of(shape):
    return lax.broadcasted_iota(jnp.int32, shape, len(shape) - 1)


def x_first(depth, start, at, own, xlow, xhigh, ylow, yhigh):
    blocks, gap = own.shape[0], DEEP - depth

    def plane(x):
        n = x - gap
        if not 0 <= n < blocks + 2 * depth:
            return None
        if n < depth:
            middle = xlow[start + n]
        elif n < depth + blocks:
            middle = own[n - depth]
        else:
            middle = xhigh[start + n - depth - blocks]
        return jnp.concatenate([ylow[at + n], middle, yhigh[at + n]], axis=0)

    return plane


def y_first(depth, start, at, own, xlow, xhigh, ylow, yhigh):
    blocks, gap = own.shape[0], DEEP - depth

    def plane(x):
        n = x - gap
        if not 0 <= n < blocks + 2 * depth:
            return None
        if n < depth:
            return xlow[start + n]
        if n >= depth + blocks:
            return xhigh[start + n - depth - blocks]
        m = n - depth
        return jnp.concatenate([ylow[at + m], own[m], yhigh[at + m]], axis=0)

    return plane


def pack_rows(parts, owns, low, high, to_high, to_low):
    start, at = 0, 0
    for depth, own in zip(parts, owns):
        blocks, rows = own.shape[0], own.shape[1]
        for first, ref, size in ((start, low, depth), (0, own, blocks), (start, high, depth)):
            to_high[at : at + size] = ref[first : first + size, rows - DEEP :, :]
            to_low[at : at + size] = ref[first : first + size, :DEEP, :]
            at += size
        start += depth


def pack_planes(parts, owns, low, high, to_high, to_low):
    start, at = 0, 0
    for depth, own in zip(parts, owns):
        blocks = own.shape[0]
        for n in range(depth):
            for first, ref in ((0, to_low), (blocks - depth, to_high)):
                m = first + n
                ref[start + n] = jnp.concatenate([low[at + m], own[m], high[at + m]], axis=0)
        start += depth
        at += blocks


def pack_ends(planes, to_high, to_low):
    groups, tall = to_high.shape[1], to_high.shape[2]
    lanes = lanes_of((tall, LANES))
    for a, plane in enumerate(planes):
        for g in range(groups):
            up = jnp.zeros((tall, LANES), jnp.float32)
            down = jnp.zeros((tall, LANES), jnp.float32)
            for i in range(GROUP):
                value = plane(g * GROUP + i)
                if value is None:
                    continue
                value = turn(value, DEEP * (i + 1))
                up = jnp.where(lanes // DEEP == i, value, up)
                down = jnp.where(lanes // DEEP == (i + 1) % GROUP, value, down)
            to_high[a, g] = up
            to_low[a, g] = down


def start_kernel(one, two, three, four, xa_high, xa_low, yb_high, yb_low):
    blocks, rows = one.shape[0], one.shape[1]
    at = 0
    for depth, own in zip(PARTS[:2], (one, two)):
        xa_high[at : at + depth] = own[blocks - depth :]
        xa_low[at : at + depth] = own[:depth]
        at += depth
    for n, own in enumerate((three, four)):
        yb_high[n * blocks : (n + 1) * blocks] = own[:, rows - DEEP :, :]
        yb_low[n * blocks : (n + 1) * blocks] = own[:, :DEEP, :]


def turn_kernel(one, two, three, four, xalow, xahigh, yblow, ybhigh, ya_high, ya_low, xb_high, xb_low):
    pack_rows(PARTS[:2], (one, two), xalow, xahigh, ya_high, ya_low)
    pack_planes(PARTS[2:], (three, four), yblow, ybhigh, xb_high, xb_low)


def planes_of(owns, halos):
    xalow, xahigh, yblow, ybhigh, yalow, yahigh, xblow, xbhigh = halos
    blocks = owns[0].shape[0]
    first = [
        x_first(PARTS[0], 0, 0, owns[0], xalow, xahigh, yalow, yahigh),
        x_first(PARTS[1], PARTS[0], blocks + 2 * PARTS[0], owns[1], xalow, xahigh, yalow, yahigh),
    ]
    return first + [
        y_first(PARTS[2], 0, 0, owns[2], xblow, xbhigh, yblow, ybhigh),
        y_first(PARTS[3], PARTS[2], blocks, owns[3], xblow, xbhigh, yblow, ybhigh),
    ]


def fill(plane, count, put):
    for x in range(count):
        value = plane(x)
        if value is not None:
            put(x, value)


def turn(plane, shift, axis=1):
    shift = shift % plane.shape[axis]
    return pltpu.roll(plane, shift, axis) if shift else plane


def unpack(low_ref, high_ref, a, put):
    groups, tall = low_ref.shape[1], low_ref.shape[2]
    lanes = lanes_of((tall, LANES))
    outer = jnp.logical_or(lanes < DEEP, lanes >= LANES - DEEP)
    for g in range(groups):
        below, above = low_ref[a, g], high_ref[a, g]
        for i in range(GROUP):
            tile = turn(jnp.where(lanes // DEEP == i, below, above), -DEEP * (i + 1))
            put(g * GROUP + i, jnp.where(outer, tile, 0.0))


def inside_mask(edge_ref, tall):
    lanes = lanes_of((tall, LANES))
    edge = edge_ref[0]
    above = jnp.logical_and(lanes < DEEP, edge != 2)
    below = jnp.logical_and(lanes >= LANES - DEEP, edge != 1)
    return jnp.where(jnp.logical_or(above, below), 1.0, 0.0)


def laplacian(ref, x, y, size, lanes):
    here = pl.ds(PAD + y, size)
    mid = [ref[t, x, here, :] for t in range(2)]
    ahead = [turn(m, -1) for m in mid]
    behind = [turn(m, 1) for m in mid]
    out = []
    for t in range(2):
        along = jnp.where(lanes == LANES - 1, ahead[1 - t], ahead[t]) + jnp.where(lanes == 0, behind[1 - t], behind[t])
        across = ref[t, x, pl.ds(PAD + y - 1, size), :] + ref[t, x, pl.ds(PAD + y + 1, size), :]
        out.append((ref[t, x - 1, here, :] + ref[t, x + 1, here, :]) + (across + along) - 6.0 * mid[t])
    return out


def build_coefficients(planes, low_ref, high_ref, mask, inv_ref, curv_ref, vel_ref):
    wide = inv_ref.shape[1]

    def keep_phase(x, tile):
        curv_ref[1, x] = tile

    def keep_vel(x, tile):
        vel_ref[1, x] = tile

    def put_phase(x, value):
        curv_ref[0, x] = value

    def put_vel(x, value):
        vel_ref[0, x] = value

    unpack(low_ref, high_ref, 2, keep_phase)
    unpack(low_ref, high_ref, 3, keep_vel)
    fill(planes[2], wide, put_phase)
    fill(planes[3], wide, put_vel)

    @pl.loop(DEEP - COEF, wide - DEEP + COEF, unroll=4)
    def _(x):
        for t in range(2):
            phase = curv_ref[t, x]
            curvature = 3.0 * phase * phase - 1.0
            inverse = 1.0 / (1.0 + diffuse_coef * 42.0 + curv_coef * 6.0 * curvature)
            inv_ref[t, x] = inverse if t == 0 else inverse * mask
            curv_ref[t, x] = curv_coef * curvature


def steps(first, last, planes, rows, size, body):
    count = (last - first) // planes

    def chunk(start, n):
        for y in range(*rows, size):
            stores = []
            for j in range(n):
                stores += body(start + j, y)
            for store in stores:
                store()

    @pl.loop(0, count)
    def _(i):
        chunk(first + i * planes, planes)

    if first + count * planes < last:
        chunk(first + count * planes, last - first - count * planes)


def writer(ref, index, value):
    def store():
        ref[index] = value

    return store


def apply_operator(u_ref, lap_ref, curv_ref, vel_ref, mask, first, last, put):
    tall = curv_ref.shape[2]
    lanes = lanes_of((CHUNK, LANES))
    mask = mask[:CHUNK]

    def lap_part(x, y):
        lap = laplacian(u_ref, x, y, CHUNK, lanes)
        lap[1] = lap[1] * mask
        return [writer(lap_ref, (t, x, pl.ds(PAD + y, CHUNK)), lap[t]) for t in range(2)]

    steps(first - 1, last + 1, PLANES, (0, tall), CHUNK, lap_part)

    def image_part(x, y):
        twice = laplacian(lap_ref, x, y, CHUNK, lanes)
        out = []
        mine, wide = pl.ds(y, CHUNK), pl.ds(PAD + y, CHUNK)
        for t in range(2):
            flow = vel_ref[t, x + 1, mine] * u_ref[t, x + 1, wide] - vel_ref[t, x - 1, mine] * u_ref[t, x - 1, wide]
            image = (u_ref[t, x, wide] + diffuse_coef * twice[t]) - (
                curv_ref[t, x, mine] * lap_ref[t, x, wide] + (0.5 * advect_coef) * flow
            )
            out += put(t, x, mine, image)
        return out

    low = first // 8 * 8
    steps(first, last, PLANES, (low, tall - low), CHUNK, image_part)


def scaled(next_ref, inv_ref, t, x, mine, value):
    return writer(next_ref, (t, x, pl.ds(PAD + mine.start, CHUNK)), inv_ref[t, x, mine] * value)


def extend_basis(k, source_ref, older_ref, u_ref, next_ref, lap_ref, inv_ref, curv_ref, vel_ref, mask, margin, keep):
    down, centre, up = recurrence(k)
    wide = inv_ref.shape[1]

    def put(t, x, mine, image):
        fresh = (image - centre * source_ref[t, x, mine]) * (1.0 / up)
        if down:
            fresh = fresh - older_ref[t, x, mine]
        stores = [writer(older_ref, (t, x, mine), fresh)]
        if (k + 1) % RESTART:
            stores.append(scaled(next_ref, inv_ref, t, x, mine, fresh))
        return stores

    apply_operator(u_ref, lap_ref, curv_ref, vel_ref, mask, margin, wide - margin, put)
    blocks, rows = keep.shape[0], keep.shape[1]
    keep[...] = older_ref[0, DEEP : DEEP + blocks, DEEP : DEEP + rows, :]


def first_half_kernel(edge_ref, *refs):
    owns, halos, (low_ref, high_ref, basis_ref), rest = refs[:4], refs[4:12], refs[12:15], refs[15:]
    a_ref, b_ref, u_ref, v_ref, lap_ref, inv_ref, curv_ref, vel_ref = rest
    wide, tall = inv_ref.shape[1], inv_ref.shape[2]
    blocks, rows = basis_ref.shape[1], basis_ref.shape[2]
    mask = inside_mask(edge_ref, tall)
    planes = planes_of(owns, halos)
    build_coefficients(planes, low_ref, high_ref, mask, inv_ref, curv_ref, vel_ref)

    def keep_start(x, tile):
        u_ref[1, x, PAD : PAD + tall] = tile * mask

    def keep_source(x, tile):
        a_ref[1, x] = tile

    def put_start(x, value):
        u_ref[0, x, PAD : PAD + tall] = value

    def put_source(x, value):
        a_ref[0, x] = value

    unpack(low_ref, high_ref, 0, keep_start)
    unpack(low_ref, high_ref, 1, keep_source)
    fill(planes[0], wide, put_start)
    fill(planes[1], wide, put_source)

    def put(t, x, mine, image):
        first = a_ref[t, x, mine] - image
        return [writer(a_ref, (t, x, mine), first), scaled(v_ref, inv_ref, t, x, mine, first)]

    apply_operator(u_ref, lap_ref, curv_ref, vel_ref, mask, 2, wide - 2, put)
    basis_ref[0] = a_ref[0, DEEP : DEEP + blocks, DEEP : DEEP + rows, :]
    here, there, now, later = a_ref, b_ref, v_ref, u_ref
    for k in range(RESTART):
        extend_basis(
            k, here, there, now, later, lap_ref, inv_ref, curv_ref, vel_ref, mask, 2 * (k + 2), basis_ref.at[k + 1]
        )
        here, there, now, later = there, here, later, now


def middle_pack_kernel(own, xlow, xhigh, ylow, yhigh, to_high, to_low):
    pack_ends([x_first(COEF, 0, 0, own, xlow, xhigh, ylow, yhigh)], to_high, to_low)


def coefficient_kernel(edge_ref, *refs):
    owns, halos, (low_ref, high_ref), (inv_ref, curv_ref, vel_ref) = refs[:4], refs[4:12], refs[12:14], refs[14:]
    mask = inside_mask(edge_ref, inv_ref.shape[2])
    build_coefficients(planes_of(owns, halos), low_ref, high_ref, mask, inv_ref, curv_ref, vel_ref)


def second_half_kernel(edge_ref, *refs):
    (inv_ref, curv_ref, vel_ref), middle, rest = refs[:3], refs[3:10], refs[10:]
    own, xlow, xhigh, ylow, yhigh, qlow_ref, qhigh_ref = middle
    older_ref, basis_ref, sums_ref, a_ref, b_ref, u_ref, v_ref, lap_ref = rest
    wide, tall = inv_ref.shape[1], inv_ref.shape[2]
    blocks, rows = older_ref.shape[1], older_ref.shape[2]
    mask = inside_mask(edge_ref, tall)

    def keep(x, tile):
        a_ref[1, x] = tile

    def put_middle(x, value):
        a_ref[0, x] = value

    unpack(qlow_ref, qhigh_ref, 0, keep)
    fill(x_first(COEF, 0, 0, own, xlow, xhigh, ylow, yhigh), wide, put_middle)

    def scale(x, y):
        return [scaled(u_ref, inv_ref, t, x, pl.ds(y, CHUNK), a_ref[t, x, pl.ds(y, CHUNK)]) for t in range(2)]

    steps(DEEP - COEF, wide - DEEP + COEF, PLANES, (0, tall), CHUNK, scale)
    here, there, now, later = a_ref, b_ref, u_ref, v_ref
    for k in range(RESTART, STEPS):
        n = k - RESTART
        extend_basis(
            k, here, there, now, later, lap_ref, inv_ref, curv_ref, vel_ref, mask, DEEP - COEF + 2 * (n + 1), basis_ref.at[n]
        )
        here, there, now, later = there, here, later, now

    def body(x, sums):
        planes = [older_ref[k, x] for k in range(RESTART + 1)] + [basis_ref[k, x] for k in range(STEPS - RESTART)]
        out = []
        for total, (i, j) in zip(sums, PAIRS):
            out.append(total + jnp.sum((planes[i] * planes[j]).reshape(rows // 8, 8, LANES), axis=0))
        return tuple(out)

    sums = lax.fori_loop(0, blocks, body, tuple(jnp.zeros((8, LANES), jnp.float32) for _ in PAIRS))
    lanes = lanes_of((8, LANES))
    packed = jnp.zeros((8, LANES), jnp.float32)
    for n, total in enumerate(sums):
        packed = jnp.where(lanes == n, jnp.sum(total, axis=1, keepdims=True), packed)
    packed = jnp.sum(packed, axis=0, keepdims=True)
    sums_ref[...] = jnp.broadcast_to(packed, sums_ref.shape)


def combine_kernel(parts_ref, older_ref, newer_ref, start_ref, phase_ref, adjoint_ref, residual_ref, sound_ref):
    blocks, rows = start_ref.shape[0], start_ref.shape[1]
    totals = jnp.sum(parts_ref[...].reshape(-1, 8, LANES), axis=0)
    totals = jnp.broadcast_to(jnp.sum(totals, axis=0, keepdims=True), (8, LANES))
    lanes = lanes_of((8, LANES))
    values = {
        pair: jnp.broadcast_to(jnp.sum(jnp.where(lanes == n, totals, 0.0), axis=1, keepdims=True), (8, LANES))
        for n, pair in enumerate(PAIRS)
    }
    gain, tail, sound = coefficients(lambda i, j: values[i, j])
    sound_ref[0] = jnp.min(sound)

    @pl.loop(0, blocks, unroll=4)
    def _(x):
        first, second = None, None
        for k in range(STEPS + 1):
            plane = (older_ref[k, x] if k <= RESTART else newer_ref[k - RESTART - 1, x]).reshape(rows // 8, 8, LANES)
            if gain[k] is not None:
                first = gain[k] * plane if first is None else first + gain[k] * plane
            second = tail[k] * plane if second is None else second + tail[k] * plane
        phase = phase_ref[x]
        curvature = 3.0 * phase * phase - 1.0
        inverse = 1.0 / (1.0 + diffuse_coef * 42.0 + curv_coef * 6.0 * curvature)
        adjoint_ref[x] = start_ref[x] + inverse * first.reshape(rows, LANES)
        residual_ref[x] = second.reshape(rows, LANES)


VMEM = pl.BlockSpec(memory_space=pltpu.VMEM)
SMEM = pl.BlockSpec(memory_space=pltpu.SMEM)


def call(kernel, outs, *args, scratch=(), scalars=0, flags=0, cost=None):
    return pl.pallas_call(
        kernel,
        out_shape=[jax.ShapeDtypeStruct(shape, jnp.float32) for shape in outs],
        in_specs=[SMEM] * scalars + [VMEM] * (len(args) - scalars),
        out_specs=[VMEM] * (len(outs) - flags) + [SMEM] * flags,
        scratch_shapes=[pltpu.VMEM(shape, jnp.float32) for shape in scratch],
        cost_estimate=cost,
        compiler_params=pltpu.CompilerParams(vmem_limit_bytes=32 * 2**20),
    )(*args)


def swapped(to_high, to_low, axis, wrap):
    peers = lax.axis_size(axis)
    up = [(i, (i + 1) % peers) for i in range(peers if wrap else peers - 1)]
    return lax.ppermute(to_high, axis, up), lax.ppermute(to_low, axis, [(j, i) for i, j in up])


def on_device(adjoint_source, start_guess, phase, velocity):
    blocks, rows, _ = phase.shape
    wide, tall = blocks + 2 * DEEP, rows + 2 * DEEP
    place = lax.axis_index("gz")
    edge = jnp.where(place == 0, 1, jnp.where(place == lax.axis_size("gz") - 1, 2, 0)).astype(jnp.int32).reshape(1)
    scratch = [(2, wide, tall + 2 * PAD * (2 <= n < 5), LANES) for n in range(8)]
    owns = [start_guess, adjoint_source, phase, velocity]

    xa, xb = sum(PARTS[:2]), sum(PARTS[2:])
    outs = ((xa, rows, LANES),) * 2 + ((2 * blocks, DEEP, LANES),) * 2
    xa_high, xa_low, yb_high, yb_low = call(start_kernel, outs, *owns)
    yb = swapped(yb_high, yb_low, "gy", True)
    halos = [*swapped(xa_high, xa_low, "gx", True), *yb]
    outs = ((2 * (blocks + xa), DEEP, LANES),) * 2 + ((xb, tall, LANES),) * 2
    ya_high, ya_low, xb_high, xb_low = call(turn_kernel, outs, *owns, *halos)
    halos += [*swapped(ya_high, ya_low, "gy", True), *swapped(xb_high, xb_low, "gx", True)]

    def pack(*refs):
        pack_ends(planes_of(refs[:4], refs[4:12]), *refs[12:])

    ends = swapped(*call(pack, ((4, wide // GROUP, tall, LANES),) * 2, *owns, *halos), "gz", False)
    known = [edge, *owns, *halos, *ends]
    (older,) = call(first_half_kernel, ((RESTART + 1, blocks, rows, LANES),), *known, scratch=scratch, scalars=1)

    held, older = lax.optimization_barrier((edge, older))
    cost = pl.CostEstimate(flops=20 * wide * tall * LANES, bytes_accessed=2**22, transcendentals=0)
    ready = call(
        coefficient_kernel, ((2, wide, tall, LANES),) * 3, held, *known[1:], scalars=1, cost=cost
    )
    middle = older[RESTART]
    xq = swapped(middle[blocks - COEF :], middle[:COEF], "gx", True)

    def pack_middle(own, low, high, to_high, to_low):
        pack_rows([COEF], [own], low, high, to_high, to_low)

    yq = swapped(*call(pack_middle, ((blocks + 2 * COEF, DEEP, LANES),) * 2, middle, *xq), "gy", True)
    zq = swapped(*call(middle_pack_kernel, ((1, wide // GROUP, tall, LANES),) * 2, middle, *xq, *yq), "gz", False)
    newer, sums = call(
        second_half_kernel,
        ((STEPS - RESTART, blocks, rows, LANES), (lax.axis_size(AXES), LANES)),
        edge, *ready, middle, *xq, *yq, *zq, older, scratch=scratch[:5], scalars=1,
    )
    parts = lax.all_to_all(sums, AXES, 0, 0, tiled=True)
    adjoint, residual, sound = call(
        combine_kernel, (phase.shape, phase.shape, (1,)), parts, older, newer, start_guess, phase, flags=1
    )

    def plain(state):
        return (jnp.float32(1.0), *plain_solve(adjoint_source, start_guess, phase, velocity))

    return lax.while_loop(lambda state: ~(state[0] > 0.5), plain, (sound[0], adjoint, residual))[1:]


def solution(mesh):
    placed = P("gx", "gy", "gz")
    return jax.shard_map(on_device, mesh=mesh, in_specs=(placed,) * 4, out_specs=(placed,) * 2, check_vma=False)
```
